128 devices in a mesh: row: 8 (over x, core), col: 16 (over y, z).
Axes of the slice: x: 4, y: 4, z: 4, core: 2. Of those that a mesh axis runs over, the one named last changes fastest.
Arguments:
- node_feats: bfloat16 [65536, 256], P(('row', 'col')), may hold values from -6 to 6
- out_grad: bfloat16 [65536, 256], P(('row', 'col')), may hold values from -6 to 6
- weight_one: bfloat16 [256, 256], replicated, may hold values from -0.375 to 0.375
- weight_two: bfloat16 [256, 256], replicated, may hold values from -0.375 to 0.375
- tile_values: bfloat16 [16384, 256, 256], P(('row', 'col')), may hold values from -0.09375 to 0.09375
- tile_rows: int32 [16384], P(('row', 'col')), may hold values from 0 to 31, as said below
- tile_cols: int32 [16384], P(('row', 'col')), may hold values from 0 to 15
- tile_count: int32 [128], P(('row', 'col')), may hold values from 1 to 128, as said below
Outputs:
- input_grad: bfloat16 [65536, 256], P(('row', 'col'))
- grad_one: float32 [256, 256], replicated
- grad_two: float32 [256, 256], replicated
The draws below stay inside these ranges and needn't reach their ends.
Inputs may be any that keep to these rules, and one draw needn't show every extreme that they name: Within one device's slots the pairs (tile_rows, tile_cols) are all different. `tile_count`: some device has all 128 slots live.
All inputs are finite; a program needn't handle non-finite values.
Results may differ from the reference program's by a relative error of at most 0.0085.
Values may be sent and summed in bfloat16 or wider, within the bound.
A program may use at most 192 MiB of HBM per device.

```python
import jax
import jax.numpy as jnp
from jax import lax

F = 256
BS = 256
BLK_DEV = 2
TILES_DEV = 128
NODES = 65536
TILES = 16384
N_ROW = 8
N_COL = 16


def tile_pattern(key):
    device_total = N_ROW * N_COL
    positions = BLK_DEV * N_COL * BLK_DEV * N_ROW
    keys = jax.random.split(key, device_total)
    chosen = jax.vmap(lambda one_key: jax.random.permutation(one_key, positions)[:TILES_DEV])(keys)
    return chosen.reshape(-1).astype(jnp.int32)


def draw_tile_rows(key, part):
    chosen = tile_pattern(key)
    return (chosen // (BLK_DEV * N_ROW)).astype(jnp.int32)


def draw_tile_cols(key, part):
    chosen = tile_pattern(key)
    return (chosen % (BLK_DEV * N_ROW)).astype(jnp.int32)


def draw_tile_count(key, part):
    key = jax.random.fold_in(key, 3)
    first_key, second_key = jax.random.split(key)
    device_total = N_ROW * N_COL
    counts = jax.random.randint(first_key, (device_total,), max(1, TILES_DEV // 8), TILES_DEV // 2 + 1)
    busiest = jax.random.randint(second_key, (), 0, device_total)
    return counts.at[busiest].set(TILES_DEV).astype(jnp.int32)


def block_levels(key, extent, shards, smallest, high):
    level = 1.0
    for axis_at, blocks in shards:
        heights = jax.random.uniform(jax.random.fold_in(jax.random.fold_in(key, 6), axis_at), (blocks,), jnp.float32, smallest / len(shards), high / len(shards))
        level = level * jnp.repeat(jnp.exp(heights), extent[axis_at] // blocks).reshape((-1,) + (1,) * (len(extent) - 1 - axis_at))
    return level


def bell_draw(own_key, shape, scale, reach, pieces=(), kind=jnp.bfloat16):
    values = scale * jax.random.normal(own_key, shape, jnp.float32)
    if pieces:
        values = values * block_levels(own_key, shape, pieces, -0.22, 0.18)
    return jnp.clip(values, -reach, reach).astype(kind)


def setup_inputs(seed: int = 0) -> dict:
    seeds = jax.random.split(jax.random.key(seed), 9)
    return {
        "node_feats": bell_draw(seeds[0], (NODES, F), 1.0, 6.0, ((0, 128),)),
        "out_grad": bell_draw(seeds[1], (NODES, F), 1.0, 6.0, ((0, 128),)),
        "weight_one": bell_draw(seeds[2], (F, F), F ** -0.5, 0.375),
        "weight_two": bell_draw(seeds[3], (F, F), F ** -0.5, 0.375),
        "tile_values": bell_draw(seeds[4], (TILES, BS, BS), (BS * 16) ** -0.5, 0.09375, ((0, 128),)),
        "tile_rows": draw_tile_rows(jax.random.fold_in(seeds[8], 71), 0),
        "tile_cols": draw_tile_cols(jax.random.fold_in(seeds[8], 71), 0),
        "tile_count": draw_tile_count(jax.random.fold_in(seeds[8], 71), 0),
    }


def sparse_product(tile_values, source_idx, target_idx, live, source, flipped):
    block_total = source.shape[0] // BS
    blocks = source.astype(jnp.float32).reshape(block_total, BS, F)
    pattern = 'tji,tjf->tif' if flipped else 'tij,tjf->tif'

    def advance(running, entry):
        values, src_blocks, dst_blocks, alive = entry
        picked = blocks[src_blocks]
        product = jnp.einsum(pattern, values.astype(jnp.float32), picked, precision=lax.Precision.HIGHEST)
        product = product * alive.astype(jnp.float32)[:, None, None]
        return running.at[dst_blocks].add(product), None

    device_total = N_ROW * N_COL
    entries = (tile_values.reshape(device_total, TILES_DEV, BS, BS),
               source_idx.reshape(device_total, TILES_DEV),
               target_idx.reshape(device_total, TILES_DEV),
               live.reshape(device_total, TILES_DEV))
    start = jnp.zeros((block_total, BS, F), jnp.float32)
    result, unused = lax.scan(advance, start, entries)
    return result.reshape(block_total * BS, F)


def reference(node_feats, out_grad, weight_one, weight_two, tile_values, tile_rows, tile_cols, tile_count):
    slot_index = jnp.arange(N_ROW * N_COL * TILES_DEV, dtype=jnp.int32)
    device_of = slot_index // TILES_DEV
    grid_row = device_of // N_COL
    grid_col = device_of % N_COL
    live = (slot_index % TILES_DEV) < tile_count[device_of]
    global_row = (grid_row * (BLK_DEV * N_COL) + tile_rows).astype(jnp.int32)
    global_col = (((tile_cols // BLK_DEV) * N_COL + grid_col) * BLK_DEV + tile_cols % BLK_DEV).astype(jnp.int32)

    projected = jnp.dot(node_feats, weight_one, preferred_element_type=jnp.float32).astype(jnp.bfloat16)
    pre_act = sparse_product(tile_values, global_col, global_row, live, projected, False)
    hidden = jax.nn.silu(pre_act).astype(jnp.bfloat16)
    back_two = sparse_product(tile_values, global_row, global_col, live, out_grad, True).astype(jnp.bfloat16)
    grad_two = jnp.dot(hidden.T, back_two, preferred_element_type=jnp.float32)
    d_hidden = jnp.dot(back_two, weight_two.T, preferred_element_type=jnp.float32)
    sigma = jax.nn.sigmoid(pre_act)
    grad_pre = (d_hidden * sigma * (1.0 + pre_act * (1.0 - sigma))).astype(jnp.bfloat16)
    back_one = sparse_product(tile_values, global_row, global_col, live, grad_pre, True).astype(jnp.bfloat16)
    grad_one = jnp.dot(node_feats.T, back_one, preferred_element_type=jnp.float32)
    input_grad = jnp.dot(back_one, weight_one.T, preferred_element_type=jnp.float32).astype(jnp.bfloat16)
    return input_grad, grad_one, grad_two
```

```python
import functools

import jax
import jax.numpy as jnp
from jax import lax
from jax.experimental import pallas as pl
from jax.experimental.pallas import tpu as pltpu
from jax.sharding import PartitionSpec as P

BF = jnp.bfloat16
F32 = jnp.float32
BS = 256
SLOTS = 128
ROW_UNITS = 32
COL_UNITS = 16
UNROLL = 8
WAYS = (1, -1)
DOT = functools.partial(jnp.dot, preferred_element_type=F32)
ROWS_OF_HALF = {1: 0, -1: 1}


class Net:
    def __init__(self, send_sems, recv_sems):
        self.send_sems, self.recv_sems = send_sems, recv_sems
        row, col = lax.axis_index("row"), lax.axis_index("col")
        self.at = {"x": row // 2, "y": col // 4, "z": col % 4}
        self.core = row % 2
        self.keys = {}
        self.started = []

    def off(self, axis, step):
        return (self.at[axis] + (step + 4)) % 4

    def peer(self, axis, step):
        at = dict(self.at)
        core = self.core
        if axis == "core":
            core = 1 - core
        else:
            at[axis] = self.off(axis, step)
        return (at["x"] * 2 + core, at["y"] * 4 + at["z"])

    def greet(self):
        barrier = pltpu.get_barrier_semaphore()
        for axis in ("x", "y", "z"):
            for way in WAYS:
                pl.semaphore_signal(
                    barrier, inc=1, device_id=self.peer(axis, way), device_id_type=pl.DeviceIdType.MESH
                )
        pl.semaphore_signal(
            barrier, inc=1, device_id=self.peer("core", 0), device_id_type=pl.DeviceIdType.MESH
        )

    def met(self):
        pl.semaphore_wait(pltpu.get_barrier_semaphore(), 7)

    def number(self, key):
        return self.keys.setdefault(key, len(self.keys))

    def copy(self, key, src, dst, axis, way):
        at = self.number(key)
        return pltpu.make_async_remote_copy(
            src_ref=src,
            dst_ref=dst,
            send_sem=self.send_sems.at[at],
            recv_sem=self.recv_sems.at[at],
            device_id=self.peer(axis, way),
            device_id_type=pl.DeviceIdType.MESH,
        )

    def send(self, key, src, dst, axis, way):
        copy = self.copy(key, src, dst, axis, way)
        copy.start()
        self.started.append(copy)

    def got(self, key, dst, axis, way):
        self.copy(key, dst, dst, axis, way).wait_recv()

    def drain(self):
        for copy in self.started:
            copy.wait_send()


class GatherPlane:
    def __init__(self, net, tag, buf):
        self.net, self.tag, self.buf = net, tag, buf
        self.half_rows = buf.shape[1] // 2

    def axes(self, block):
        return ("y", "z") if block == 0 else ("z", "y")

    def unit(self, block, first, second):
        one, two = self.axes(block)
        at = {one: self.net.off(one, first), two: self.net.off(two, second)}
        return (at["y"] * 4 + at["z"]) * 2 + block

    def whole(self, block, first, second):
        return self.buf.at[self.unit(block, first, second)]

    def half(self, block, first, second, way):
        rows = pl.ds(ROWS_OF_HALF[way] * self.half_rows, self.half_rows)
        return self.buf.at[self.unit(block, first, second), rows]

    def put(self, key, ref, axis, way):
        self.net.send((self.tag, *key), ref, ref, axis, way)

    def get(self, key, ref, axis, way):
        self.net.got((self.tag, *key), ref, axis, way)

    def spread(self, block, first):
        two = self.axes(block)[1]
        for way in WAYS:
            self.put(("c", block, first, way), self.whole(block, first, 0), two, way)

    def start(self):
        for block in (0, 1):
            one = self.axes(block)[0]
            for way in WAYS:
                self.put(("a", block, way), self.whole(block, 0, 0), one, way)
        for block in (0, 1):
            self.spread(block, 0)

    def step1(self):
        for way in WAYS:
            for block in (0, 1):
                one = self.axes(block)[0]
                self.get(("a", block, way), self.whole(block, -way, 0), one, way)
                self.put(("f", block, way), self.half(block, -way, 0, way), one, way)
                self.spread(block, -way)

    def pass_on(self, first):
        for block in (0, 1):
            two = self.axes(block)[1]
            for way in WAYS:
                self.get(("c", block, first, way), self.whole(block, first, -way), two, way)
                self.put(("e", block, first, way), self.half(block, first, -way, way), two, way)

    def step2(self):
        self.pass_on(0)

    def step3(self):
        for block in (0, 1):
            one = self.axes(block)[0]
            for way in WAYS:
                self.get(("f", block, way), self.half(block, 2, 0, way), one, way)
            self.spread(block, 2)

    def step4(self):
        self.pass_on(-1)
        self.pass_on(1)

    def step5(self):
        self.pass_on(2)

    def finish(self):
        for first in (0, -1, 1, 2):
            for block in (0, 1):
                two = self.axes(block)[1]
                for way in WAYS:
                    self.get(("e", block, first, way), self.half(block, first, 2, way), two, way)


class GatherLine:
    def __init__(self, net, tag, buf):
        self.net, self.tag, self.buf = net, tag, buf

    def first(self, step, core):
        return (self.net.off("x", step) * 2 + core) * 2

    def pair(self, step, other=False):
        core = 1 - self.net.core if other else self.net.core
        return self.buf.at[pl.ds(self.first(step, core), 2)]

    def half(self, step, way):
        return self.buf.at[self.first(step, self.net.core) + ROWS_OF_HALF[way]]

    def share(self, step):
        self.net.send((self.tag, "s", step), self.pair(step), self.pair(step), "core", 0)

    def start(self):
        for way in WAYS:
            self.net.send((self.tag, "a", way), self.pair(0), self.pair(0), "x", way)
        self.share(0)

    def step1(self):
        for way in WAYS:
            self.net.got((self.tag, "a", way), self.pair(-way), "x", way)
            ref = self.half(-way, way)
            self.net.send((self.tag, "f", way), ref, ref, "x", way)
            self.share(-way)

    def step2(self):
        for way in WAYS:
            self.net.got((self.tag, "f", way), self.half(2, way), "x", way)
        self.share(2)

    def finish(self):
        for step in (0, -1, 1, 2):
            self.net.got((self.tag, "s", step), self.pair(step, other=True), "core", 0)


class RingSum:
    def __init__(self, net, tag, axis, half, relay, landed):
        self.net, self.tag, self.axis = net, tag, axis
        self.half, self.relay, self.landed = half, relay, landed

    def start(self):
        for way in WAYS:
            self.net.send(
                (self.tag, "p", way), self.half(2, ROWS_OF_HALF[way]), self.relay[way], self.axis, way
            )

    def start_near(self):
        for way in WAYS:
            rest = 1 - ROWS_OF_HALF[way]
            self.net.send(
                (self.tag, "q", way), self.half(way, rest), self.landed[way][rest], self.axis, way
            )

    def middle(self):
        for way in WAYS:
            turn = ROWS_OF_HALF[way]
            self.net.got((self.tag, "p", way), self.relay[way], self.axis, way)
            mine = self.half(way, turn)
            mine[...] = (mine[...].astype(F32) + self.relay[way][...].astype(F32)).astype(BF)
            self.net.send((self.tag, "r", way), mine, self.landed[way][turn], self.axis, way)

    def finish(self, h, own=None):
        total = (self.half(0, h)[...] if own is None else own).astype(F32)
        for way in WAYS:
            kind = "r" if ROWS_OF_HALF[way] == h else "q"
            self.net.got((self.tag, kind, way), self.landed[way][h], self.axis, way)
            total = total + self.landed[way][h][...].astype(F32)
        return total


class LineSum:
    def __init__(self, net, tag, part, swapped, relay, landed):
        self.net, self.tag, self.part, self.swapped = net, tag, part, swapped
        self.ring = RingSum(
            net,
            (tag, "ring"),
            "x",
            lambda step, h: part.at[self.first(step, net.core) + h],
            {1: relay.at[0], -1: relay.at[1]},
            {1: [landed.at[0], landed.at[1]], -1: [landed.at[2], landed.at[3]]},
        )

    def first(self, step, core):
        return (self.net.off("x", step) * 2 + core) * 2

    def there(self, step):
        return self.swapped.at[pl.ds(self.net.off("x", step) * 2, 2)]

    def start(self):
        for step in (2, 1, -1, 0):
            src = self.part.at[pl.ds(self.first(step, 1 - self.net.core), 2)]
            self.net.send((self.tag, "s", step), src, self.there(step), "core", 0)

    def join(self, step):
        self.net.got((self.tag, "s", step), self.there(step), "core", 0)
        for h in (0, 1):
            mine = self.part.at[self.first(step, self.net.core) + h]
            other = self.swapped.at[self.net.off("x", step) * 2 + h]
            mine[...] = (mine[...].astype(F32) + other[...].astype(F32)).astype(BF)

    def middle(self):
        self.join(2)
        self.ring.start()
        self.join(1)
        self.join(-1)
        self.ring.start_near()
        self.join(0)

    def late(self):
        self.ring.middle()

    def finish(self, h):
        return self.ring.finish(h)


class PlaneSum:
    ORDER = (2, 1, -1, 0)

    def __init__(self, net, tag, part, relay, landed, part2, relay2, landed2):
        self.net, self.part, self.part2 = net, part, part2
        rows = part.shape[1] // 2
        cut = [pl.ds(0, rows), pl.ds(rows, rows)]
        self.cut = cut
        self.rings, self.last = {}, {}
        for block in (0, 1):
            one, two = ("z", "y") if block == 0 else ("y", "z")

            def unit(first, second, block=block, one=one, two=two):
                at = {one: net.off(one, first), two: net.off(two, second)}
                return (at["y"] * 4 + at["z"]) * 2 + block

            for k, second in enumerate(self.ORDER):
                base = (block * 4 + k) * 2
                self.rings[block, k] = RingSum(
                    net,
                    (tag, "one", block, k),
                    one,
                    lambda step, h, unit=unit, second=second: part.at[unit(step, second), cut[h]],
                    {1: relay.at[base], -1: relay.at[base + 1]},
                    {
                        1: [landed.at[base, cut[h]] for h in (0, 1)],
                        -1: [landed.at[base + 1, cut[h]] for h in (0, 1)],
                    },
                )
            base = block * 2
            self.last[block] = RingSum(
                net,
                (tag, "two", block),
                two,
                lambda step, h, block=block: part2.at[block * 4 + self.ORDER.index(step), cut[h]],
                {1: relay2.at[base], -1: relay2.at[base + 1]},
                {
                    1: [landed2.at[base, cut[h]] for h in (0, 1)],
                    -1: [landed2.at[base + 1, cut[h]] for h in (0, 1)],
                },
            )

    def start(self, k):
        for block in (0, 1):
            self.rings[block, k].start()
        for block in (0, 1):
            self.rings[block, k].start_near()

    def middle(self, k):
        for block in (0, 1):
            self.rings[block, k].middle()

    def close(self, k):
        for block in (0, 1):
            for h in (0, 1):
                total = self.rings[block, k].finish(h)
                self.part2[block * 4 + k, self.cut[h]] = total.astype(BF)
        if k == 0:
            for block in (0, 1):
                self.last[block].start()
        if k == 2:
            for block in (0, 1):
                self.last[block].start_near()

    def late(self):
        for block in (0, 1):
            self.last[block].middle()

    def finish(self, block, h):
        return self.last[block].finish(h)


def products(count, begin, left, right, keep, total, sums):
    def body(step, carry):
        for turn in range(UNROLL):
            t = begin + step * UNROLL + turn
            value = total[...] * keep(t) + DOT(left(t), right(t))
            total[...] = value
            sums[t] = value.astype(BF)
        return carry

    lax.fori_loop(0, count // UNROLL, body, 0)


def pick(units, sums, last, some, part):
    def body(u, carry):
        part[u] = (sums[last(u)].astype(F32) * some(u)).astype(BF)
        return carry

    lax.fori_loop(0, units, body, 0)


def both(values):
    high = values.astype(BF)
    return high, (values - high.astype(F32)).astype(BF)


NT = (((1,), (1,)), ((), ()))


def front_kernel(
    plan, feats, cot, w_one, w_two, tiles_hbm, grad_pre, grad_one, grad_two,
    tiles, sums, total, feats_all, cot_all, part, relay, landed, part2, relay2, landed2,
    part_x, swapped, relay_x, landed_x, w_one_t, tile_sem, send_sems, recv_sems,
):
    net = Net(send_sems, recv_sems)
    net.greet()
    load = pltpu.make_async_copy(tiles_hbm, tiles, tile_sem)
    load.start()
    line = GatherLine(net, "x", feats_all)
    plane = GatherPlane(net, "g", cot_all)
    for block in (0, 1):
        rows = pl.ds(block * BS, BS)
        feats_all[line.first(0, net.core) + block] = feats[rows]
        cot_all[plane.unit(block, 0, 0)] = cot[rows].astype(F32).T.astype(BF)
    net.met()
    line.start()
    plane.start()
    w_one_t[...] = w_one[...].astype(F32).T.astype(BF)
    total[...] = jnp.zeros_like(total)
    line.step1()
    plane.step1()
    line.step2()
    plane.step2()
    plane.step3()
    line.finish()
    load.wait()

    def ahead(count, begin):
        products(
            count,
            begin,
            lambda t: tiles[plan[0, t]],
            lambda t: feats_all[plan[1, t]],
            lambda t: plan[2, t].astype(F32),
            total,
            sums,
        )

    ahead(64, 0)
    plane.step4()
    ahead(64, 64)
    plane.step5()
    pick(ROW_UNITS, sums, lambda u: plan[6, u], lambda u: plan[6, u + 32].astype(F32), part)
    plane_sum = PlaneSum(net, "ax", part, relay, landed, part2, relay2, landed2)
    for k in range(4):
        plane_sum.start(k)
    plane.finish()
    total[...] = jnp.zeros_like(total)
    products(
        SLOTS,
        0,
        lambda t: cot_all[plan[4, t]],
        lambda t: tiles[plan[3, t]],
        lambda t: plan[5, t].astype(F32),
        total,
        sums,
    )
    pick(COL_UNITS, sums, lambda u: plan[6, u + 64], lambda u: plan[6, u + 96].astype(F32), part_x)
    line_sum = LineSum(net, "bt", part_x, swapped, relay_x, landed_x)
    line_sum.start()
    plane_sum.middle(0)
    plane_sum.middle(1)
    plane_sum.middle(2)
    plane_sum.middle(3)
    line_sum.middle()
    plane_sum.close(0)
    line_sum.late()
    plane_sum.close(1)
    plane_sum.close(2)
    plane_sum.close(3)
    plane_sum.late()
    back = [line_sum.finish(block).astype(BF) for block in (0, 1)]
    d_hidden = [DOT(w_two[...], back[block]) for block in (0, 1)]
    one = jnp.zeros((BS, BS), F32)
    two = jnp.zeros((BS, BS), F32)
    for block in (0, 1):
        ax = jnp.concatenate([plane_sum.finish(block, h) for h in (0, 1)], axis=0).T
        high, low = both(ax)
        pre = DOT(w_one_t[...], high) + DOT(w_one_t[...], low)
        gate = 1.0 / (1.0 + jnp.exp(-pre))
        hidden = (pre * gate).astype(BF)
        slope = (d_hidden[block] * gate * (1.0 + pre * (1.0 - gate))).astype(BF)
        grad_pre[block] = slope
        two += lax.dot_general(hidden, back[block], NT, preferred_element_type=F32)
        one += lax.dot_general(high, slope, NT, preferred_element_type=F32)
        one += lax.dot_general(low, slope, NT, preferred_element_type=F32)
    grad_one[...] = one
    grad_two[...] = two
    net.drain()


def back_kernel(
    plan, grad_pre, w_one, tiles_hbm, input_grad,
    tiles, sums, total, grad_all_0, grad_all_1, part_0, swapped_0, relay_0, landed_0,
    part_1, swapped_1, relay_1, landed_1, result, tile_sem, send_sems, recv_sems,
):
    net = Net(send_sems, recv_sems)
    net.greet()
    load = pltpu.make_async_copy(tiles_hbm, tiles, tile_sem)
    load.start()
    half = BS // 2
    gathers, scatters = [], []
    for h, (buf, *scratch) in enumerate(
        (
            (grad_all_0, part_0, swapped_0, relay_0, landed_0),
            (grad_all_1, part_1, swapped_1, relay_1, landed_1),
        )
    ):
        gathers.append(GatherPlane(net, ("p", h), buf))
        scatters.append(LineSum(net, ("s", h), *scratch))
        for block in (0, 1):
            buf[gathers[h].unit(block, 0, 0)] = grad_pre[block, pl.ds(h * half, half)]
    net.met()
    total[...] = jnp.zeros_like(total)
    early, late = gathers
    early.start()
    early.step1()
    early.step2()
    early.step3()
    early.step4()
    late.start()
    early.step5()
    late.step1()
    late.step2()
    early.finish()
    load.wait()

    def run(count, begin, buf):
        products(
            count,
            begin,
            lambda t: buf[plan[4, t]],
            lambda t: tiles[plan[3, t]],
            lambda t: plan[5, t].astype(F32),
            total,
            sums,
        )

    def choose(part):
        pick(COL_UNITS, sums, lambda u: plan[6, u + 64], lambda u: plan[6, u + 96].astype(F32), part)

    def apply(h):
        for block in (0, 1):
            back = scatters[h].finish(block).astype(BF)
            value = DOT(w_one[:, h * half : (h + 1) * half], back)
            if h == 0:
                result[block] = value
            else:
                input_grad[pl.ds(block * BS, BS)] = (result[block] + value).T.astype(BF)

    run(64, 0, grad_all_0)
    late.step3()
    run(64, 64, grad_all_0)
    late.step4()
    choose(part_0)
    scatters[0].start()
    late.step5()
    scatters[0].middle()
    scatters[0].late()
    apply(0)
    late.finish()
    total[...] = jnp.zeros_like(total)
    run(SLOTS, 0, grad_all_1)
    choose(part_1)
    scatters[1].start()
    scatters[1].middle()
    scatters[1].late()
    apply(1)
    net.drain()


def in_order(major, minor, live):
    slots = jnp.arange(SLOTS, dtype=jnp.int32)
    key = jnp.where(live, major * 64 + minor, 4096 + slots)
    rank = jnp.sum((key[None, :] < key[:, None]).astype(jnp.int32), axis=1)
    at = rank[:, None] == slots[None, :]
    order = jnp.sum(jnp.where(at, slots[:, None], 0), axis=0)
    minors = jnp.sum(jnp.where(at, minor[:, None], 0), axis=0)
    majors = jnp.sum(jnp.where(at, jnp.where(live, major, -1)[:, None], 0), axis=0)
    keep = jnp.concatenate([jnp.zeros((1,), jnp.int32), (majors[1:] == majors[:-1]).astype(jnp.int32)])
    return order, minors, keep


def ends(major, live, units):
    unit = jnp.arange(units, dtype=jnp.int32)[:, None]
    before = jnp.sum(((major[None, :] <= unit) & live[None, :]).astype(jnp.int32), axis=1)
    some = jnp.any((major[None, :] == unit) & live[None, :], axis=1)
    pad = jnp.zeros((32 - units,), jnp.int32)
    return [jnp.maximum(before - 1, 0), pad, some.astype(jnp.int32), pad]


def make_plan(tile_rows, tile_cols, tile_count):
    live = jnp.arange(SLOTS, dtype=jnp.int32) < tile_count[0]
    rows, cols = jnp.clip(tile_rows, 0, ROW_UNITS - 1), jnp.clip(tile_cols, 0, COL_UNITS - 1)
    last = jnp.concatenate(ends(rows, live, ROW_UNITS) + ends(cols, live, COL_UNITS))
    none = jnp.zeros((SLOTS,), jnp.int32)
    return jnp.stack([*in_order(rows, cols, live), *in_order(cols, rows, live), last, none])


def units(count, rows=BS):
    return pltpu.VMEM((count, rows, BS), BF)


SMEM = pl.BlockSpec(memory_space=pltpu.SMEM)
VMEM = pl.BlockSpec(memory_space=pltpu.VMEM)
ANY = pl.BlockSpec(memory_space=pl.ANY)


def front(plan, feats, cot, w_one, w_two, tiles):
    half = BS // 2
    return pl.pallas_call(
        front_kernel,
        out_shape=(
            jax.ShapeDtypeStruct((2, BS, BS), BF),
            jax.ShapeDtypeStruct((BS, BS), F32),
            jax.ShapeDtypeStruct((BS, BS), F32),
        ),
        in_specs=[SMEM, VMEM, VMEM, VMEM, VMEM, ANY],
        out_specs=(VMEM, VMEM, VMEM),
        scratch_shapes=[
            units(SLOTS),
            units(SLOTS),
            pltpu.VMEM((BS, BS), F32),
            units(COL_UNITS),
            units(ROW_UNITS),
            units(ROW_UNITS),
            units(16, half),
            units(16),
            units(8),
            units(4, half),
            units(4),
            units(COL_UNITS),
            units(8),
            units(2),
            units(4),
            pltpu.VMEM((BS, BS), BF),
            pltpu.SemaphoreType.DMA,
            pltpu.SemaphoreType.DMA((120,)),
            pltpu.SemaphoreType.DMA((120,)),
        ],
        compiler_params=pltpu.CompilerParams(
            collective_id=0, has_side_effects=True, vmem_limit_bytes=60 * 2**20
        ),
        name="front",
    )(plan, feats, cot, w_one, w_two, tiles)


def back(plan, grad_pre, w_one, tiles):
    half = BS // 2
    sums = [units(COL_UNITS, half), units(8, half), units(2, half), units(4, half)]
    return pl.pallas_call(
        back_kernel,
        out_shape=jax.ShapeDtypeStruct((2 * BS, BS), BF),
        in_specs=[SMEM, VMEM, VMEM, ANY],
        out_specs=VMEM,
        scratch_shapes=[
            units(SLOTS),
            units(SLOTS, half),
            pltpu.VMEM((half, BS), F32),
            units(ROW_UNITS, half),
            units(ROW_UNITS, half),
            *sums,
            *sums,
            pltpu.VMEM((2, BS, BS), F32),
            pltpu.SemaphoreType.DMA,
            pltpu.SemaphoreType.DMA((120,)),
            pltpu.SemaphoreType.DMA((120,)),
        ],
        compiler_params=pltpu.CompilerParams(
            collective_id=1, has_side_effects=True, vmem_limit_bytes=60 * 2**20
        ),
        name="back",
    )(plan, grad_pre, w_one, tiles)


def per_device(
    node_feats, out_grad, weight_one, weight_two, tile_values, tile_rows, tile_cols, tile_count
):
    plan = make_plan(tile_rows, tile_cols, tile_count)
    grad_pre, grad_one, grad_two = front(plan, node_feats, out_grad, weight_one, weight_two, tile_values)
    grads = lax.psum(jnp.concatenate([grad_one, grad_two], axis=0), ("row", "col"))
    input_grad = back(plan, grad_pre, weight_one, tile_values)
    return (input_grad, grads[:BS], grads[BS:])


def solution(mesh):
    in_specs = (
        P(("row", "col"), None),
        P(("row", "col"), None),
        P(),
        P(),
        P(("row", "col"), None, None),
        P(("row", "col")),
        P(("row", "col")),
        P(("row", "col")),
    )
    out_specs = (P(("row", "col"), None), P(), P())
    return jax.shard_map(
        per_device, mesh=mesh, in_specs=in_specs, out_specs=out_specs, check_vma=False
    )
```

```python
import functools

import jax
import jax.numpy as jnp
from jax import lax
from jax.experimental import pallas as pl
from jax.experimental.pallas import tpu as pltpu
from jax.sharding import PartitionSpec as P

BF = jnp.bfloat16
F32 = jnp.float32
BS = 256
SLOTS = 128
ROW_UNITS = 32
COL_UNITS = 16
UNROLL = 16
WAYS = (1, -1)
DOT = functools.partial(jnp.dot, preferred_element_type=F32)
ROWS_OF_HALF = {1: 0, -1: 1}
PARTNERS = [(axis, step) for axis in ("x", "y", "z") for step in (1, -1, 2)] + [("core", 0)]


class Net:
    def __init__(self, sems):
        self.sems = sems
        row, col = lax.axis_index("row"), lax.axis_index("col")
        self.at = {"x": row // 2, "y": col // 4, "z": col % 4}
        self.core = row % 2
        self.keys = {}

    def off(self, axis, step):
        return (self.at[axis] + (step + 4)) % 4

    def peer(self, axis, step):
        at = dict(self.at)
        core = self.core
        if axis == "core":
            core = 1 - core
        else:
            at[axis] = self.off(axis, step)
        return (at["x"] * 2 + core, at["y"] * 4 + at["z"])

    def greet(self):
        barrier = pltpu.get_barrier_semaphore()
        for axis, way in PARTNERS:
            pl.semaphore_signal(
                barrier, inc=1, device_id=self.peer(axis, way), device_id_type=pl.DeviceIdType.MESH
            )

    def met(self):
        pl.semaphore_wait(pltpu.get_barrier_semaphore(), len(PARTNERS))

    def copy(self, leave, land, src, dst, axis, way):
        at = [self.keys.setdefault(key, len(self.keys)) for key in (("out", leave), ("in", land))]
        return pltpu.make_async_remote_copy(
            src_ref=src,
            dst_ref=dst,
            send_sem=self.sems.at[at[0]],
            recv_sem=self.sems.at[at[1]],
            device_id=self.peer(axis, way),
            device_id_type=pl.DeviceIdType.MESH,
        )

    def send(self, leave, land, src, dst, axis, way):
        self.copy(leave, land, src, dst, axis, way).start()

    def got(self, leave, land, ref):
        self.copy(leave, land, ref, ref, "core", 0).wait_recv()

    def left(self, leave, land, ref):
        self.copy(leave, land, ref, ref, "core", 0).wait_send()


class GatherPlane:
    def __init__(self, net, tag, buf):
        self.net, self.tag, self.buf = net, tag, buf
        self.half_rows = buf.shape[1] // 2

    def axes(self, block):
        return ("y", "z") if block == 0 else ("z", "y")

    def unit(self, block, first, second):
        one, two = self.axes(block)
        at = {one: self.net.off(one, first), two: self.net.off(two, second)}
        return (at["y"] * 4 + at["z"]) * 2 + block

    def whole(self, block, first, second):
        return self.buf.at[self.unit(block, first, second)]

    def half(self, block, first, second, way):
        rows = pl.ds(ROWS_OF_HALF[way] * self.half_rows, self.half_rows)
        return self.buf.at[self.unit(block, first, second), rows]

    def put(self, key, ref, axis, way):
        self.net.send(self.tag, (self.tag, *key), ref, ref, axis, way)

    def get(self, key, count):
        self.net.got(self.tag, (self.tag, *key), self.buf.at[pl.ds(0, count)])

    def spread(self, block, first):
        two = self.axes(block)[1]
        for way in WAYS:
            self.put(("c", first), self.whole(block, first, 0), two, way)

    def start(self):
        for block in (0, 1):
            one = self.axes(block)[0]
            for way in WAYS:
                self.put(("a",), self.whole(block, 0, 0), one, way)

    def start_more(self):
        for block in (0, 1):
            self.spread(block, 0)

    def step1(self):
        self.get(("a",), 4)
        for block in (0, 1):
            one = self.axes(block)[0]
            for way in WAYS:
                self.put(("f",), self.half(block, -way, 0, way), one, way)
        for way in WAYS:
            for block in (0, 1):
                self.spread(block, -way)

    def pass_on(self, first):
        self.get(("c", first), 4)
        for block in (0, 1):
            two = self.axes(block)[1]
            for way in WAYS:
                self.put(("e",), self.half(block, first, -way, way), two, way)

    def step2(self):
        self.pass_on(0)

    def step3(self):
        self.get(("f",), 2)
        for block in (0, 1):
            self.spread(block, 2)

    def step4(self):
        self.pass_on(-1)
        self.pass_on(1)

    def step5(self):
        self.pass_on(2)

    def finish(self):
        self.get(("e",), 8)

    def left(self):
        self.net.left(self.tag, (self.tag, "a"), self.buf.at[pl.ds(0, 30)])


class GatherLine:
    def __init__(self, net, tag, buf):
        self.net, self.tag, self.buf = net, tag, buf

    def first(self, step, core):
        return (self.net.off("x", step) * 2 + core) * 2

    def get(self, kind, count):
        self.net.got(self.tag, (self.tag, kind), self.buf.at[pl.ds(0, count)])

    def share(self, step):
        ref = self.buf.at[pl.ds(self.first(step, self.net.core), 2)]
        self.net.send(self.tag, (self.tag, "s"), ref, ref, "core", 0)

    def pass_half(self, kind, step, h, way):
        ref = self.buf.at[self.first(step, self.net.core) + h]
        self.net.send(self.tag, (self.tag, kind), ref, ref, "x", way)

    def start(self):
        for way in WAYS:
            self.pass_half("a", 0, ROWS_OF_HALF[way], way)

    def start_more(self):
        for way in WAYS:
            self.pass_half("b", 0, 1 - ROWS_OF_HALF[way], way)
        self.share(0)

    def step1(self):
        self.get("a", 2)
        for way in WAYS:
            self.pass_half("f", -way, ROWS_OF_HALF[way], way)

    def step2(self):
        self.get("b", 2)
        for way in WAYS:
            self.share(-way)

    def step3(self):
        self.get("f", 2)
        self.share(2)

    def finish(self):
        self.get("s", 8)

    def left(self):
        self.net.left(self.tag, (self.tag, "a"), self.buf.at[pl.ds(0, 14)])


class RingSum:
    def __init__(self, net, tag, keys, axis, half, relay, landed, more=None):
        self.net, self.tag, self.keys, self.axis = net, tag, keys, axis
        self.half, self.relay, self.landed, self.more = half, relay, landed, more

    def send(self, at, src, dst, way):
        self.net.send(self.tag, self.keys[at], src, dst, self.axis, way)

    def term(self, step, h):
        value = self.half(step, h)[...].astype(F32)
        return value if self.more is None else value + self.more(step, h)[...].astype(F32)

    def start(self):
        for way in WAYS:
            self.send(0, self.half(2, ROWS_OF_HALF[way]), self.relay[way], way)

    def start_near(self):
        for way in WAYS:
            rest = 1 - ROWS_OF_HALF[way]
            self.send(1, self.half(way, rest), self.landed[way][rest], way)

    def middle(self):
        for way in WAYS:
            turn = ROWS_OF_HALF[way]
            mine = self.half(way, turn)
            mine[...] = (self.term(way, turn) + self.relay[way][...].astype(F32)).astype(BF)
            self.send(1, mine, self.landed[way][turn], way)

    def finish(self, h):
        total = self.term(0, h)
        for way in WAYS:
            total = total + self.landed[way][h][...].astype(F32)
        return total


class LineSum:
    def __init__(self, net, tag, part, swapped, relay, landed):
        self.net, self.tag, self.part, self.swapped = net, tag, part, swapped
        self.relay, self.landed = relay, landed
        self.ring = RingSum(
            net,
            tag,
            ((tag, "p"), (tag, "n")),
            "x",
            lambda step, h: part.at[self.first(step, net.core) + h],
            {1: relay.at[0], -1: relay.at[1]},
            {1: [landed.at[0], landed.at[1]], -1: [landed.at[2], landed.at[3]]},
            lambda step, h: swapped.at[net.off("x", step) * 2 + h],
        )

    def first(self, step, core):
        return (self.net.off("x", step) * 2 + core) * 2

    def get(self, kind, ref):
        self.net.got(self.tag, (self.tag, kind), ref)

    def start(self):
        for step in (2, 1, -1, 0):
            src = self.part.at[pl.ds(self.first(step, 1 - self.net.core), 2)]
            dst = self.swapped.at[pl.ds(self.net.off("x", step) * 2, 2)]
            self.net.send(self.tag, (self.tag, "s" if step == 2 else "u"), src, dst, "core", 0)

    def join(self, step, h):
        self.part[self.first(step, self.net.core) + h] = self.ring.term(step, h).astype(BF)

    def middle(self):
        self.get("s", self.swapped.at[pl.ds(0, 2)])
        self.join(2, 0)
        self.join(2, 1)
        self.ring.start()

    def middle_more(self):
        self.get("u", self.swapped.at[pl.ds(0, 6)])
        for way in WAYS:
            self.join(way, 1 - ROWS_OF_HALF[way])
        self.ring.start_near()

    def late(self):
        self.get("p", self.relay)
        self.ring.middle()

    def arrive(self):
        self.get("n", self.landed)

    def finish(self, h):
        return self.ring.finish(h)

    def left(self):
        self.net.left(self.tag, (self.tag, "s"), self.part.at[pl.ds(0, 14)])


class PlaneSum:
    ORDER = (2, 1, -1, 0)

    def __init__(self, net, tag, part, relay, landed, part2, relay2, landed2):
        self.net, self.tag, self.part, self.part2 = net, tag, part, part2
        rows = part.shape[1] // 2
        cut = [pl.ds(0, rows), pl.ds(rows, rows)]
        self.cut = cut
        self.rings, self.last = {}, {}
        for block in (0, 1):
            one, two = ("z", "y") if block == 0 else ("y", "z")

            def unit(first, second, block=block, one=one, two=two):
                at = {one: net.off(one, first), two: net.off(two, second)}
                return (at["y"] * 4 + at["z"]) * 2 + block

            for k, second in enumerate(self.ORDER):
                base = (block * 4 + k) * 2
                self.rings[block, k] = RingSum(
                    net,
                    tag,
                    ((tag, "p", k), (tag, "n", k)),
                    one,
                    lambda step, h, unit=unit, second=second: part.at[unit(step, second), cut[h]],
                    {1: relay.at[base], -1: relay.at[base + 1]},
                    {
                        1: [landed.at[base, cut[h]] for h in (0, 1)],
                        -1: [landed.at[base + 1, cut[h]] for h in (0, 1)],
                    },
                )
            base = block * 2
            self.last[block] = RingSum(
                net,
                tag,
                ((tag, "p", 4), (tag, "n", 4)),
                two,
                lambda step, h, block=block: part2.at[block * 4 + self.ORDER.index(step), cut[h]],
                {1: relay2.at[base], -1: relay2.at[base + 1]},
                {
                    1: [landed2.at[base, cut[h]] for h in (0, 1)],
                    -1: [landed2.at[base + 1, cut[h]] for h in (0, 1)],
                },
            )

    def get(self, kind, k, count):
        self.net.got(self.tag, (self.tag, kind, k), self.part.at[pl.ds(0, count)])

    def start(self, k):
        for block in (0, 1):
            self.rings[block, k].start()

    def start_near(self, k):
        for block in (0, 1):
            self.rings[block, k].start_near()

    def middle(self, k):
        self.get("p", k, 2)
        for block in (0, 1):
            self.rings[block, k].middle()

    def close(self, k):
        self.get("n", k, 4)
        for block in (0, 1):
            for h in (0, 1):
                self.part2[block * 4 + k, self.cut[h]] = self.rings[block, k].finish(h).astype(BF)
        if k == 0:
            for block in (0, 1):
                self.last[block].start()
        if k == 2:
            for block in (0, 1):
                self.last[block].start_near()

    def late(self):
        self.get("p", 4, 2)
        for block in (0, 1):
            self.last[block].middle()

    def arrive(self):
        self.get("n", 4, 4)

    def finish(self, block, h):
        return self.last[block].finish(h)

    def left(self):
        self.net.left(self.tag, (self.tag, "p", 0), self.part.at[pl.ds(0, 30)])


class GradSum:
    FAR = (1, -1, 2)

    def __init__(self, net, mine, swapped, from_x, from_y, from_z, done):
        self.net, self.mine, self.swapped, self.done = net, mine, swapped, done
        self.from_x, self.from_y, self.from_z = from_x, from_y, from_z

    def rows(self, *steps):
        size = {1: 256, 2: 64, 3: 16}[len(steps)]
        at = ((1 - self.net.core) if steps[0] else self.net.core) * 256
        for axis, step, span in zip(("x", "y"), steps[1:], (64, 16)):
            at = at + self.net.off(axis, step) * span
        return pl.ds(pl.multiple_of(at, size), size)

    def put(self, stage, src, dst, axis, step):
        self.net.send(("w", axis), ("w", stage), src, dst, axis, step)

    def get(self, stage, ref):
        self.net.got(("w", "core"), ("w", stage), ref)

    def start(self):
        self.put(0, self.mine.at[self.rows(1)], self.swapped, "core", 0)

    def step1(self):
        self.get(0, self.swapped)
        rows = self.rows(0)
        self.mine[rows] = self.mine[rows] + self.swapped[...]
        for k, step in enumerate(self.FAR):
            self.put(1, self.mine.at[self.rows(0, step)], self.from_x.at[k], "x", step)

    def step2(self):
        self.get(1, self.from_x)
        rows = self.rows(0, 0)
        self.mine[rows] = (self.mine[rows] + self.from_x[0]) + (self.from_x[1] + self.from_x[2])
        for k, step in enumerate(self.FAR):
            self.put(2, self.mine.at[self.rows(0, 0, step)], self.from_y.at[k], "y", step)

    def step3(self):
        self.get(2, self.from_y)
        ref = self.from_z.at[self.net.at["z"]]
        ref[...] = (self.mine[self.rows(0, 0, 0)] + self.from_y[0]) + (self.from_y[1] + self.from_y[2])
        for step in self.FAR:
            self.put(3, ref, ref, "z", step)

    def step4(self):
        self.get(3, self.from_z.at[pl.ds(0, 3)])
        ref = self.done.at[self.rows(0, 0, 0)]
        ref[...] = (self.from_z[0] + self.from_z[1]) + (self.from_z[2] + self.from_z[3])
        for step in self.FAR:
            self.put(4, ref, ref, "y", step)

    def step5(self):
        self.get(4, self.done.at[pl.ds(0, 48)])
        ref = self.done.at[self.rows(0, 0)]
        for step in self.FAR:
            self.put(5, ref, ref, "x", step)

    def step6(self):
        self.get(5, self.done.at[pl.ds(0, 192)])
        ref = self.done.at[self.rows(0)]
        self.put(6, ref, ref, "core", 0)

    def finish(self):
        self.get(6, self.swapped)

    def left(self):
        for axis, rows in (("core", 512), ("x", 384), ("y", 96), ("z", 48)):
            self.net.left(("w", axis), ("w", 0), self.done.at[pl.ds(0, rows)])


def within(index, count):
    return jnp.clip(index, 0, count - 1)


def products(count, begin, left, right, keep, total, sums):
    def body(step, carry):
        for turn in range(UNROLL):
            t = begin + step * UNROLL + turn
            value = total[...] * keep(t) + DOT(left(t), right(t))
            total[...] = value
            sums[t] = value.astype(BF)
        return carry

    lax.fori_loop(0, count // UNROLL, body, 0)


def pick(units, sums, last, some, part):
    def body(u, carry):
        part[u] = (sums[last(u)].astype(F32) * some(u)).astype(BF)
        return carry

    lax.fori_loop(0, units, body, 0)


def both(values):
    high = values.astype(BF)
    return high, (values - high.astype(F32)).astype(BF)


NT = (((1,), (1,)), ((), ()))


def kernel(
    rows, cols, count, feats, cot, w_one, w_two, tiles_hbm, back_out, grads_out,
    plan, plan_wide, tiles, sums, total, feats_all, cot_all, part, relay, landed, part2, relay2, landed2,
    part_x, swapped, relay_x, landed_x, w_one_t,
    slope_all_0, swapped_0, relay_0, landed_0,
    slope_all_1, swapped_1, relay_1, landed_1,
    mine, swapped_w, from_x, from_y, from_z, done, tile_sem, plan_sem, sems,
):
    net = Net(sems)
    net.greet()
    load = pltpu.make_async_copy(tiles_hbm, tiles, tile_sem)
    load.start()
    line = GatherLine(net, "x", feats_all)
    plane = GatherPlane(net, "g", cot_all)
    for block in (0, 1):
        span = pl.ds(block * BS, BS)
        feats_all[line.first(0, net.core) + block] = feats[span]
        cot_all[plane.unit(block, 0, 0)] = cot[span].astype(F32).T.astype(BF)
    net.met()
    line.start()
    plane.start()
    write_plan(rows, cols, count[0], plan_wide)
    to_plan = pltpu.make_async_copy(plan_wide, plan, plan_sem)
    to_plan.start()
    w_one_t[...] = w_one[...].astype(F32).T.astype(BF)
    total[...] = jnp.zeros_like(total)
    line.start_more()
    plane.start_more()
    line.step1()
    plane.step1()
    line.step2()
    plane.step2()
    line.step3()
    line.finish()
    load.wait()
    to_plan.wait()

    def ahead(count, begin):
        products(
            count,
            begin,
            lambda t: tiles[within(plan[0, t], SLOTS)],
            lambda t: feats_all[within(plan[1, t], COL_UNITS)],
            lambda t: plan[2, t].astype(F32),
            total,
            sums,
        )

    def back(count, begin, left, rows):
        products(
            count,
            begin,
            lambda t: left[within(plan[4, t], ROW_UNITS)],
            lambda t: tiles[within(plan[3, t], SLOTS)],
            lambda t: plan[5, t].astype(F32),
            total.at[pl.ds(0, rows)],
            sums.at[:, pl.ds(0, rows)],
        )

    def choose(to, rows):
        pick(
            COL_UNITS,
            sums.at[:, pl.ds(0, rows)],
            lambda u: within(plan[8, u], SLOTS),
            lambda u: plan[9, u].astype(F32),
            to,
        )

    ahead(64, 0)
    plane.step3()
    ahead(64, 64)
    plane.step4()
    pick(ROW_UNITS, sums, lambda u: within(plan[6, u], SLOTS), lambda u: plan[7, u].astype(F32), part)
    plane_sum = PlaneSum(net, "ax", part, relay, landed, part2, relay2, landed2)
    plane.step5()
    for k in range(4):
        plane_sum.start(k)
    for k in range(4):
        plane_sum.start_near(k)
    total[...] = jnp.zeros_like(total)
    plane.finish()
    back(SLOTS, 0, cot_all, BS)
    choose(part_x, BS)
    line_sum = LineSum(net, "bt", part_x, swapped, relay_x, landed_x)
    line_sum.start()
    plane_sum.middle(0)
    plane_sum.middle(1)
    line_sum.middle()
    plane_sum.middle(2)
    line_sum.middle_more()
    plane_sum.middle(3)
    plane_sum.close(0)
    line_sum.late()
    plane_sum.close(1)
    plane_sum.close(2)
    plane_sum.close(3)
    plane_sum.late()
    line_sum.arrive()
    plane_sum.arrive()
    half = BS // 2
    early = GatherPlane(net, "p", slope_all_0)
    late = GatherPlane(net, "q", slope_all_1)
    ax_parts, hiddens, grads, back_two = [], [], [], []
    for block in (0, 1):
        back_two.append(line_sum.finish(block).astype(BF))
        d_hidden = DOT(w_two[...], back_two[block])
        ax = jnp.concatenate([plane_sum.finish(block, h) for h in (0, 1)], axis=0).T
        high, low = both(ax)
        pre = DOT(w_one_t[...], high) + DOT(w_one_t[...], low)
        gate = 1.0 / (1.0 + jnp.exp(-pre))
        slope = (d_hidden * gate * (1.0 + pre * (1.0 - gate))).astype(BF)
        grads.append(slope)
        slope_all_0[early.unit(block, 0, 0)] = slope[:half]
        slope_all_1[late.unit(block, 0, 0)] = slope[half:]
        hiddens.append((pre * gate).astype(BF))
        ax_parts.append((high, low))
    early.start()
    total[...] = jnp.zeros_like(total)
    one = jnp.zeros((BS, BS), F32)
    two = jnp.zeros((BS, BS), F32)
    for block in (0, 1):
        two += lax.dot_general(hiddens[block], back_two[block], NT, preferred_element_type=F32)
        for values in ax_parts[block]:
            one += lax.dot_general(values, grads[block], NT, preferred_element_type=F32)
    mine[:BS] = one
    mine[BS:] = two
    early.start_more()
    weights = GradSum(net, mine, swapped_w, from_x, from_y, from_z, done)
    weights.start()
    late.start()
    early.step1()
    early.step2()
    late.start_more()
    early.step3()
    weights.step1()
    early.step4()
    late.step1()
    early.step5()
    late.step2()
    early.finish()
    weights.step2()
    back(64, 0, slope_all_0, half)
    late.step3()
    back(64, 64, slope_all_0, half)
    late.step4()
    line_sum.left()
    part_0, part_1 = (part_x.at[:, pl.ds(h * half, half)] for h in (0, 1))
    choose(part_0, half)
    first = LineSum(net, "s", part_0, swapped_0, relay_0, landed_0)
    second = LineSum(net, "t", part_1, swapped_1, relay_1, landed_1)
    first.start()
    late.step5()
    weights.step3()
    total[...] = jnp.zeros_like(total)
    first.middle()
    first.middle_more()
    late.finish()
    weights.step4()
    back(64, 0, slope_all_1, half)
    first.late()
    back(64, 64, slope_all_1, half)
    choose(part_1, half)
    second.start()
    weights.step5()
    second.middle()
    first.arrive()
    for block in (0, 1):
        back_out[block, :half] = first.finish(block).astype(BF)
    second.middle_more()
    second.late()
    weights.step6()
    for copies in (line, plane, plane_sum, early, late, first):
        copies.left()
    second.arrive()
    for block in (0, 1):
        back_out[block, half:] = second.finish(block).astype(BF)
    weights.finish()
    grads_out[...] = done[...]
    second.left()
    weights.left()


def finish_kernel(back, w_one, grads, input_grad, grad_one, grad_two):
    grad_one[...] = grads[:BS]
    grad_two[...] = grads[BS:]
    for block in (0, 1):
        input_grad[pl.ds(block * BS, BS)] = DOT(w_one[...], back[block]).T.astype(BF)


def write_plan(rows, cols, count, plan):
    shape = (SLOTS, SLOTS)
    down = lax.broadcasted_iota(jnp.int32, shape, 0)
    across = lax.broadcasted_iota(jnp.int32, shape, 1)
    live = down < count

    def tall(ref, top):
        return jnp.broadcast_to(jnp.clip(ref[...], 0, top), shape).T

    def over_slots(where, values):
        return jnp.sum(jnp.where(where, values, 0), axis=0, keepdims=True)

    rows, cols = tall(rows, ROW_UNITS - 1), tall(cols, COL_UNITS - 1)
    for at, last_at, major, minor in ((0, 6, rows, cols), (3, 8, cols, rows)):
        key = jnp.where(live, major * 64 + minor, 4096 + down)
        rank = jnp.sum(jnp.where(key.T < key, 1, 0), axis=1, keepdims=True)
        here = rank == across
        alive = jnp.where(live, major, -1)
        plan[at : at + 1] = over_slots(here, down)
        plan[at + 1 : at + 2] = over_slots(here, minor)
        same = over_slots(here, alive) == over_slots(rank + 1 == across, alive)
        plan[at + 2 : at + 3] = jnp.where(same & (across[:1] > 0), 1, 0)
        plan[last_at : last_at + 1] = jnp.maximum(over_slots(live & (major <= across), 1) - 1, 0)
        plan[last_at + 1 : last_at + 2] = jnp.minimum(over_slots(live & (major == across), 1), 1)


def units(count, rows=BS):
    return pltpu.VMEM((count, rows, BS), BF)


SMEM = pl.BlockSpec(memory_space=pltpu.SMEM)
VMEM = pl.BlockSpec(memory_space=pltpu.VMEM)
ANY = pl.BlockSpec(memory_space=pl.ANY)


def call(rows, cols, count, feats, cot, w_one, w_two, tiles):
    half = BS // 2
    last = [units(ROW_UNITS, half), units(8, half), units(2, half), units(4, half)]
    return pl.pallas_call(
        kernel,
        out_shape=(
            jax.ShapeDtypeStruct((2, BS, BS), BF),
            jax.ShapeDtypeStruct((2 * BS, BS), F32),
        ),
        in_specs=[VMEM, VMEM, SMEM, VMEM, VMEM, VMEM, VMEM, ANY],
        out_specs=(VMEM, VMEM),
        scratch_shapes=[
            pltpu.SMEM((16, SLOTS), jnp.int32),
            pltpu.VMEM((16, SLOTS), jnp.int32),
            units(SLOTS),
            units(SLOTS),
            pltpu.VMEM((BS, BS), F32),
            units(COL_UNITS),
            units(ROW_UNITS),
            units(ROW_UNITS),
            units(16, half),
            units(16),
            units(8),
            units(4, half),
            units(4),
            units(COL_UNITS),
            units(8),
            units(2),
            units(4),
            pltpu.VMEM((BS, BS), BF),
            *last,
            *last,
            pltpu.VMEM((2 * BS, BS), F32),
            pltpu.VMEM((BS, BS), F32),
            pltpu.VMEM((3, 64, BS), F32),
            pltpu.VMEM((3, 16, BS), F32),
            pltpu.VMEM((4, 16, BS), F32),
            pltpu.VMEM((2 * BS, BS), F32),
            pltpu.SemaphoreType.DMA,
            pltpu.SemaphoreType.DMA,
            pltpu.SemaphoreType.DMA((67,)),
        ],
        compiler_params=pltpu.CompilerParams(
            collective_id=0, has_side_effects=True, vmem_limit_bytes=62 * 2**20
        ),
        name="graph_back",
    )(rows, cols, count, feats, cot, w_one, w_two, tiles)


def per_device(
    node_feats, out_grad, weight_one, weight_two, tile_values, tile_rows, tile_cols, tile_count
):
    back, grads = call(
        tile_rows.reshape(1, SLOTS),
        tile_cols.reshape(1, SLOTS),
        tile_count,
        node_feats,
        out_grad,
        weight_one,
        weight_two,
        tile_values,
    )
    return pl.pallas_call(
        finish_kernel,
        out_shape=(
            jax.ShapeDtypeStruct((2 * BS, BS), BF),
            jax.ShapeDtypeStruct((BS, BS), F32),
            jax.ShapeDtypeStruct((BS, BS), F32),
        ),
        in_specs=[VMEM, VMEM, VMEM],
        out_specs=(VMEM, VMEM, VMEM),
        name="finish",
    )(back, weight_one, grads)


def solution(mesh):
    in_specs = (
        P(("row", "col"), None),
        P(("row", "col"), None),
        P(),
        P(),
        P(("row", "col"), None, None),
        P(("row", "col")),
        P(("row", "col")),
        P(("row", "col")),
    )
    out_specs = (P(("row", "col"), None), P(), P())
    return jax.shard_map(
        per_device, mesh=mesh, in_specs=in_specs, out_specs=out_specs, check_vma=False
    )
```

```python
import functools

import jax
import jax.numpy as jnp
from jax import lax
from jax.experimental import pallas as pl
from jax.experimental.pallas import tpu as pltpu
from jax.sharding import PartitionSpec as P

BF = jnp.bfloat16
F32 = jnp.float32
BS = 256
SLOTS = 128
ROW_UNITS = 32
COL_UNITS = 16
UNROLL = 16
EARLY = 128
WAYS = (1, -1)
DOT = functools.partial(jnp.dot, preferred_element_type=F32)
ROWS_OF_HALF = {1: 0, -1: 1}
PARTNERS = [(axis, step) for axis in ("x", "y", "z") for step in (1, -1, 2)] + [("core", 0)]


class Net:
    def __init__(self, sems):
        self.sems = sems
        row, col = lax.axis_index("row"), lax.axis_index("col")
        self.at = {"x": row // 2, "y": col // 4, "z": col % 4}
        self.core = row % 2
        self.keys = {}

    def off(self, axis, step):
        return (self.at[axis] + (step + 4)) % 4

    def peer(self, axis, step):
        at = dict(self.at)
        core = self.core
        if axis == "core":
            core = 1 - core
        else:
            at[axis] = self.off(axis, step)
        return (at["x"] * 2 + core, at["y"] * 4 + at["z"])

    def greet(self):
        barrier = pltpu.get_barrier_semaphore()
        for axis, way in PARTNERS:
            pl.semaphore_signal(
                barrier, inc=1, device_id=self.peer(axis, way), device_id_type=pl.DeviceIdType.MESH
            )

    def met(self):
        pl.semaphore_wait(pltpu.get_barrier_semaphore(), len(PARTNERS))

    def copy(self, leave, land, src, dst, axis, way):
        at = [self.keys.setdefault(key, len(self.keys)) for key in (("out", leave), ("in", land))]
        return pltpu.make_async_remote_copy(
            src_ref=src,
            dst_ref=dst,
            send_sem=self.sems.at[at[0]],
            recv_sem=self.sems.at[at[1]],
            device_id=self.peer(axis, way),
            device_id_type=pl.DeviceIdType.MESH,
        )

    def send(self, leave, land, src, dst, axis, way):
        self.copy(leave, land, src, dst, axis, way).start()

    def got(self, leave, land, ref):
        self.copy(leave, land, ref, ref, "core", 0).wait_recv()

    def left(self, leave, land, ref):
        self.copy(leave, land, ref, ref, "core", 0).wait_send()


class GatherPlane:
    def __init__(self, net, tag, buf):
        self.net, self.tag, self.buf = net, tag, buf
        self.half_rows = buf.shape[1] // 2

    def axes(self, block):
        return ("y", "z") if block == 0 else ("z", "y")

    def unit(self, block, first, second):
        one, two = self.axes(block)
        at = {one: self.net.off(one, first), two: self.net.off(two, second)}
        return (at["y"] * 4 + at["z"]) * 2 + block

    def whole(self, block, first, second):
        return self.buf.at[self.unit(block, first, second)]

    def half(self, block, first, second, way):
        rows = pl.ds(ROWS_OF_HALF[way] * self.half_rows, self.half_rows)
        return self.buf.at[self.unit(block, first, second), rows]

    def put(self, key, ref, axis, way):
        leave = (self.tag, "a" if key == ("a",) else "rest")
        self.net.send(leave, (self.tag, *key), ref, ref, axis, way)

    def get(self, key, count):
        self.net.got((self.tag, "a"), (self.tag, *key), self.buf.at[pl.ds(0, count)])

    def spread(self, block, first):
        two = self.axes(block)[1]
        for way in WAYS:
            self.put(("c", first), self.whole(block, first, 0), two, way)

    def start(self):
        for block in (0, 1):
            one = self.axes(block)[0]
            for way in WAYS:
                self.put(("a",), self.whole(block, 0, 0), one, way)

    def start_more(self):
        for block in (0, 1):
            self.spread(block, 0)

    def step1(self):
        self.get(("a",), 4)
        for block in (0, 1):
            one = self.axes(block)[0]
            for way in WAYS:
                self.put(("f",), self.half(block, -way, 0, way), one, way)
        for way in WAYS:
            for block in (0, 1):
                self.spread(block, -way)

    def pass_on(self, first):
        self.get(("c", first), 4)
        for block in (0, 1):
            two = self.axes(block)[1]
            for way in WAYS:
                self.put(("e",), self.half(block, first, -way, way), two, way)

    def step2(self):
        self.pass_on(0)

    def step3(self):
        self.get(("f",), 2)
        for block in (0, 1):
            self.spread(block, 2)

    def step4(self):
        self.pass_on(-1)
        self.pass_on(1)

    def step5(self):
        self.pass_on(2)

    def finish(self):
        self.get(("e",), 8)

    def left_first(self):
        self.net.left((self.tag, "a"), (self.tag, "a"), self.buf.at[pl.ds(0, 4)])

    def left(self):
        self.net.left((self.tag, "rest"), (self.tag, "a"), self.buf.at[pl.ds(0, 26)])


class GatherLine:
    def __init__(self, net, tag, buf):
        self.net, self.tag, self.buf = net, tag, buf

    def first(self, step, core):
        return (self.net.off("x", step) * 2 + core) * 2

    def get(self, kind, count):
        self.net.got(self.tag, (self.tag, kind), self.buf.at[pl.ds(0, count)])

    def share(self, step):
        ref = self.buf.at[pl.ds(self.first(step, self.net.core), 2)]
        self.net.send(self.tag, (self.tag, "s"), ref, ref, "core", 0)

    def pass_half(self, kind, step, h, way):
        ref = self.buf.at[self.first(step, self.net.core) + h]
        self.net.send(self.tag, (self.tag, kind), ref, ref, "x", way)

    def start(self):
        for way in WAYS:
            self.pass_half("a", 0, ROWS_OF_HALF[way], way)

    def start_more(self):
        for way in WAYS:
            self.pass_half("b", 0, 1 - ROWS_OF_HALF[way], way)
        self.share(0)

    def step1(self):
        self.get("a", 2)
        for way in WAYS:
            self.pass_half("f", -way, ROWS_OF_HALF[way], way)

    def step2(self):
        self.get("b", 2)
        for way in WAYS:
            self.share(-way)

    def step3(self):
        self.get("f", 2)
        self.share(2)

    def finish(self):
        self.get("s", 8)

    def left(self):
        self.net.left(self.tag, (self.tag, "a"), self.buf.at[pl.ds(0, 14)])


class RingSum:
    def __init__(self, net, tag, keys, axis, half, relay, landed, more=None):
        self.net, self.tag, self.keys, self.axis = net, tag, keys, axis
        self.half, self.relay, self.landed, self.more = half, relay, landed, more

    def send(self, at, src, dst, way):
        self.net.send((self.tag, at), self.keys[at], src, dst, self.axis, way)

    def term(self, step, h):
        value = self.half(step, h)[...].astype(F32)
        return value if self.more is None else value + self.more(step, h)[...].astype(F32)

    def start(self):
        for way in WAYS:
            self.send(0, self.half(2, ROWS_OF_HALF[way]), self.relay[way], way)

    def start_near(self):
        for way in WAYS:
            rest = 1 - ROWS_OF_HALF[way]
            self.send(1, self.half(way, rest), self.landed[way][rest], way)

    def middle(self):
        for way in WAYS:
            turn = ROWS_OF_HALF[way]
            mine = self.half(way, turn)
            mine[...] = (self.term(way, turn) + self.relay[way][...].astype(F32)).astype(BF)
            self.send(1, mine, self.landed[way][turn], way)

    def finish(self, h):
        total = self.term(0, h)
        for way in WAYS:
            total = total + self.landed[way][h][...].astype(F32)
        return total


class LineSum:
    def __init__(self, net, tag, part, swapped, relay, landed):
        self.net, self.tag, self.part, self.swapped = net, tag, part, swapped
        self.relay, self.landed = relay, landed
        self.ring = RingSum(
            net,
            tag,
            ((tag, "p"), (tag, "n")),
            "x",
            lambda step, h: part.at[self.first(step, net.core) + h],
            {1: relay.at[0], -1: relay.at[1]},
            {1: [landed.at[0], landed.at[1]], -1: [landed.at[2], landed.at[3]]},
            lambda step, h: swapped.at[net.off("x", step) * 2 + h],
        )

    def first(self, step, core):
        return (self.net.off("x", step) * 2 + core) * 2

    def get(self, kind, ref):
        self.net.got((self.tag, 0), (self.tag, kind), ref)

    def start(self):
        for step in (2, 1, -1, 0):
            src = self.part.at[pl.ds(self.first(step, 1 - self.net.core), 2)]
            dst = self.swapped.at[pl.ds(self.net.off("x", step) * 2, 2)]
            self.net.send((self.tag, 1), (self.tag, "s" if step == 2 else "u"), src, dst, "core", 0)

    def join(self, step, h):
        self.part[self.first(step, self.net.core) + h] = self.ring.term(step, h).astype(BF)

    def middle(self):
        self.get("s", self.swapped.at[pl.ds(0, 2)])
        self.join(2, 0)
        self.join(2, 1)
        self.ring.start()

    def middle_more(self):
        self.get("u", self.swapped.at[pl.ds(0, 6)])
        for way in WAYS:
            self.join(way, 1 - ROWS_OF_HALF[way])

    def near(self):
        self.net.left((self.tag, 0), (self.tag, "s"), self.relay)
        self.ring.start_near()

    def late(self):
        self.get("p", self.relay)
        self.ring.middle()

    def arrive(self):
        self.get("n", self.landed)

    def finish(self, h):
        return self.ring.finish(h)

    def left(self):
        self.net.left((self.tag, 1), (self.tag, "s"), self.part.at[pl.ds(0, 12)])


class PlaneSum:
    ORDER = (2, 1, -1, 0)

    def __init__(self, net, tag, part, relay, landed, part2, relay2, landed2):
        self.net, self.tag, self.part, self.part2 = net, tag, part, part2
        rows = part.shape[1] // 2
        cut = [pl.ds(0, rows), pl.ds(rows, rows)]
        self.cut = cut
        self.rings, self.last = {}, {}
        for block in (0, 1):
            one, two = ("z", "y") if block == 0 else ("y", "z")

            def unit(first, second, block=block, one=one, two=two):
                at = {one: net.off(one, first), two: net.off(two, second)}
                return (at["y"] * 4 + at["z"]) * 2 + block

            for k, second in enumerate(self.ORDER):
                base = (block * 4 + k) * 2
                self.rings[block, k] = RingSum(
                    net,
                    tag,
                    ((tag, "p", k), (tag, "n", k)),
                    one,
                    lambda step, h, unit=unit, second=second: part.at[unit(step, second), cut[h]],
                    {1: relay.at[base], -1: relay.at[base + 1]},
                    {
                        1: [landed.at[base, cut[h]] for h in (0, 1)],
                        -1: [landed.at[base + 1, cut[h]] for h in (0, 1)],
                    },
                )
            base = block * 2
            self.last[block] = RingSum(
                net,
                tag,
                ((tag, "p", 4), (tag, "n", 4)),
                two,
                lambda step, h, block=block: part2.at[block * 4 + self.ORDER.index(step), cut[h]],
                {1: relay2.at[base], -1: relay2.at[base + 1]},
                {
                    1: [landed2.at[base, cut[h]] for h in (0, 1)],
                    -1: [landed2.at[base + 1, cut[h]] for h in (0, 1)],
                },
            )

    def get(self, kind, k, count):
        self.net.got((self.tag, 0), (self.tag, kind, k), self.part.at[pl.ds(0, count)])

    def start(self, k):
        for block in (0, 1):
            self.rings[block, k].start()

    def start_near(self, k):
        for block in (0, 1):
            self.rings[block, k].start_near()

    def middle(self, k):
        self.get("p", k, 2)
        for block in (0, 1):
            self.rings[block, k].middle()

    def close(self, k):
        self.get("n", k, 4)
        for block in (0, 1):
            for h in (0, 1):
                self.part2[block * 4 + k, self.cut[h]] = self.rings[block, k].finish(h).astype(BF)
        if k == 0:
            for block in (0, 1):
                self.last[block].start()
        if k == 2:
            for block in (0, 1):
                self.last[block].start_near()

    def late(self):
        self.get("p", 4, 2)
        for block in (0, 1):
            self.last[block].middle()

    def arrive(self):
        self.get("n", 4, 4)

    def finish(self, block, h):
        return self.last[block].finish(h)

    def left(self):
        self.net.left((self.tag, 0), (self.tag, "p", 0), self.part.at[pl.ds(0, 10)])
        self.net.left((self.tag, 1), (self.tag, "p", 0), self.part.at[pl.ds(0, 20)])


class GradSum:
    FAR = (1, -1, 2)

    def __init__(self, net, mine, swapped, from_x, from_y, from_z, done):
        self.net, self.mine, self.swapped, self.done = net, mine, swapped, done
        self.from_x, self.from_y, self.from_z = from_x, from_y, from_z

    def rows(self, *steps):
        size = {1: 256, 2: 64, 3: 16}[len(steps)]
        at = ((1 - self.net.core) if steps[0] else self.net.core) * 256
        for axis, step, span in zip(("x", "y"), steps[1:], (64, 16)):
            at = at + self.net.off(axis, step) * span
        return pl.ds(pl.multiple_of(at, size), size)

    def put(self, stage, src, dst, axis, step):
        self.net.send(("w", axis), ("w", stage), src, dst, axis, step)

    def get(self, stage, ref):
        self.net.got(("w", "core"), ("w", stage), ref)

    def start(self):
        self.put(0, self.mine.at[self.rows(1)], self.swapped, "core", 0)

    def step1(self):
        self.get(0, self.swapped)
        rows = self.rows(0)
        self.mine[rows] = self.mine[rows] + self.swapped[...]
        for k, step in enumerate(self.FAR):
            self.put(1, self.mine.at[self.rows(0, step)], self.from_x.at[k], "x", step)

    def step2(self):
        self.get(1, self.from_x)
        rows = self.rows(0, 0)
        self.mine[rows] = (self.mine[rows] + self.from_x[0]) + (self.from_x[1] + self.from_x[2])
        for k, step in enumerate(self.FAR):
            self.put(2, self.mine.at[self.rows(0, 0, step)], self.from_y.at[k], "y", step)

    def step3(self):
        self.get(2, self.from_y)
        ref = self.from_z.at[self.net.at["z"]]
        ref[...] = (self.mine[self.rows(0, 0, 0)] + self.from_y[0]) + (self.from_y[1] + self.from_y[2])
        for step in self.FAR:
            self.put(3, ref, ref, "z", step)

    def step4(self):
        self.get(3, self.from_z.at[pl.ds(0, 3)])
        at = self.net.at
        ref = self.done.at[self.net.core, at["x"], at["y"]]
        ref[...] = (self.from_z[0] + self.from_z[1]) + (self.from_z[2] + self.from_z[3])
        for step in self.FAR:
            self.put(4, ref, ref, "x", step)

    def step5(self):
        self.get(4, self.from_y)
        ref = self.done.at[self.net.core, :, self.net.at["y"]]
        for step in self.FAR:
            self.put(5, ref, ref, "y", step)

    def step6(self):
        self.get(5, self.from_x)
        ref = self.done.at[self.net.core]
        self.put(6, ref, ref, "core", 0)

    def finish(self):
        self.get(6, self.swapped)

    def left(self):
        for axis, rows in (("core", 512), ("x", 240), ("y", 240), ("z", 48)):
            self.net.left(("w", axis), ("w", 0), self.mine.at[pl.ds(0, rows)])


def within(index, count):
    return jnp.clip(index, 0, count - 1)


def products(count, begin, left, right, keep, total, sums, unroll=UNROLL):
    def body(step, carry):
        for turn in range(unroll):
            t = begin + step * unroll + turn
            value = total[...] * keep(t) + DOT(left(t), right(t))
            total[...] = value
            sums[t] = value.astype(BF)
        return carry

    lax.fori_loop(0, count // unroll, body, 0)


def pick(units, sums, last, some, part):
    def body(u, carry):
        part[u] = (sums[last(u)].astype(F32) * some(u)).astype(BF)
        return carry

    lax.fori_loop(0, units, body, 0)


def both(values):
    high = values.astype(BF)
    return high, (values - high.astype(F32)).astype(BF)


NT = (((1,), (1,)), ((), ()))


def kernel(
    rows_in, cols_in, count, feats, cot_in, w_one_in, w_two_in, tiles_hbm, back_out, grads_out,
    rows, cols, cot, w_one, w_two, plan, plan_wide, tiles, sums, total, feats_all, cot_all, part, relay, landed, part2, relay2, landed2,
    part_x, swapped, relay_x, landed_x, w_one_t,
    slope_all_0, swapped_0, relay_0, landed_0,
    slope_all_1, swapped_1, relay_1, landed_1,
    mine, swapped_w, from_x, from_y, from_z, done, tile_sem, plan_sem, cot_sem, feats_sem, small_sem, grads_sem, sems,
):
    net = Net(sems)
    net.greet()
    line = GatherLine(net, "x", feats_all)
    plane = GatherPlane(net, "g", cot_all)
    loads = [pltpu.make_async_copy(cot_in, cot, cot_sem)]
    for block in (0, 1):
        span = pl.ds(block * BS, BS)
        own = feats_all.at[line.first(0, net.core) + block]
        loads.append(pltpu.make_async_copy(feats.at[span], own, feats_sem.at[block]))
    for at, (src, dst) in enumerate(((rows_in, rows), (cols_in, cols), (w_one_in, w_one), (w_two_in, w_two))):
        loads.append(pltpu.make_async_copy(src, dst, small_sem.at[at]))
    loads.append(pltpu.make_async_copy(tiles_hbm, tiles, tile_sem))
    for load in loads:
        load.start()
    loads[0].wait()
    for block in (0, 1):
        span = pl.ds(block * BS, BS)
        cot_all[plane.unit(block, 0, 0)] = cot[span].astype(F32).T.astype(BF)
    for load in loads[1:-1]:
        load.wait()
    w_one_t[...] = w_one[...].astype(F32).T.astype(BF)
    total[...] = jnp.zeros_like(total)
    write_plan(rows, cols, count[0], plan_wide)
    to_plan = pltpu.make_async_copy(plan_wide, plan, plan_sem)
    to_plan.start()
    net.met()
    line.start()
    plane.start()
    line.start_more()
    plane.start_more()
    line.step1()
    plane.step1()
    line.step2()
    plane.step2()
    line.step3()
    line.finish()
    loads[-1].wait()
    to_plan.wait()

    def ahead(count, begin):
        products(
            count,
            begin,
            lambda t: tiles[within(plan[0, t], SLOTS)],
            lambda t: feats_all[within(plan[1, t], COL_UNITS)],
            lambda t: plan[2, t].astype(F32),
            total,
            sums,
        )

    def back(count, begin, left, rows, unroll=UNROLL):
        products(
            count,
            begin,
            lambda t: left[within(plan[4, t], ROW_UNITS)],
            lambda t: tiles[within(plan[3, t], SLOTS)],
            lambda t: plan[5, t].astype(F32),
            total.at[pl.ds(0, rows)],
            sums.at[:, pl.ds(0, rows)],
            unroll,
        )

    def choose(to, rows):
        pick(
            COL_UNITS,
            sums.at[:, pl.ds(0, rows)],
            lambda u: within(plan[8, u], SLOTS),
            lambda u: plan[9, u].astype(F32),
            to,
        )

    ahead(64, 0)
    plane.step3()
    ahead(64, 64)
    plane.step4()
    pick(ROW_UNITS, sums, lambda u: within(plan[6, u], SLOTS), lambda u: plan[7, u].astype(F32), part)
    plane_sum = PlaneSum(net, "ax", part, relay, landed, part2, relay2, landed2)
    plane.step5()
    for k in range(4):
        plane_sum.start(k)
    for k in range(4):
        plane_sum.start_near(k)
    total[...] = jnp.zeros_like(total)
    plane.finish()
    back(SLOTS, 0, cot_all, BS)
    choose(part_x, BS)
    line_sum = LineSum(net, "bt", part_x, swapped, relay_x, landed_x)
    line_sum.start()
    plane_sum.middle(0)
    plane_sum.middle(1)
    line_sum.middle()
    plane_sum.middle(2)
    line_sum.middle_more()
    plane_sum.middle(3)
    line_sum.near()
    plane_sum.close(0)
    line_sum.late()
    plane_sum.close(1)
    plane_sum.close(2)
    plane_sum.close(3)
    plane_sum.late()
    line_sum.arrive()
    plane_sum.arrive()
    early = GatherPlane(net, "p", slope_all_0)
    late = GatherPlane(net, "q", slope_all_1)
    ax_parts, hiddens, grads, back_two = [], [], [], []
    for block in (0, 1):
        back_two.append(line_sum.finish(block).astype(BF))
        d_hidden = DOT(w_two[...], back_two[block])
        ax = jnp.concatenate([plane_sum.finish(block, h) for h in (0, 1)], axis=0).T
        high, low = both(ax)
        pre = DOT(w_one_t[...], high) + DOT(w_one_t[...], low)
        gate = 1.0 / (1.0 + jnp.exp(-pre))
        slope = (d_hidden * gate * (1.0 + pre * (1.0 - gate))).astype(BF)
        grads.append(slope)
        slope_all_0[early.unit(block, 0, 0)] = slope[:EARLY]
        slope_all_1[late.unit(block, 0, 0)] = slope[EARLY:]
        hiddens.append((pre * gate).astype(BF))
        ax_parts.append((high, low))
    early.start()
    total[...] = jnp.zeros_like(total)
    one = jnp.zeros((BS, BS), F32)
    two = jnp.zeros((BS, BS), F32)
    for block in (0, 1):
        two += lax.dot_general(hiddens[block], back_two[block], NT, preferred_element_type=F32)
        for values in ax_parts[block]:
            one += lax.dot_general(values, grads[block], NT, preferred_element_type=F32)
    mine[:BS] = one
    mine[BS:] = two
    weights = GradSum(net, mine, swapped_w, from_x, from_y, from_z, done)
    weights.start()
    early.left_first()
    early.start_more()
    late.start()
    weights.step1()
    early.step1()
    early.step2()
    weights.step2()
    late.start_more()
    early.step3()
    early.step4()
    late.step1()
    early.step5()
    weights.step3()
    late.step2()
    late.step3()
    late.step4()
    early.finish()
    back(32, 0, slope_all_0, EARLY, 32)
    late.step5()
    weights.step4()
    back(96, 32, slope_all_0, EARLY, 32)
    weights.step5()
    line_sum.left()
    part_0, part_1 = part_x.at[:, pl.ds(0, EARLY)], part_x.at[:, pl.ds(EARLY, BS - EARLY)]
    choose(part_0, EARLY)
    first = LineSum(net, "s", part_0, swapped_0, relay_0, landed_0)
    second = LineSum(net, "t", part_1, swapped_1, relay_1, landed_1)
    first.start()
    total[...] = jnp.zeros_like(total)
    late.finish()
    back(32, 0, slope_all_1, BS - EARLY, 32)
    first.middle()
    first.middle_more()
    back(96, 32, slope_all_1, BS - EARLY, 32)
    first.near()
    choose(part_1, BS - EARLY)
    second.start()
    first.late()
    weights.step6()
    second.middle()
    second.middle_more()
    second.near()
    weights.finish()
    keep = pltpu.make_async_copy(done, grads_out, grads_sem)
    keep.start()
    first.arrive()
    for block in (0, 1):
        back_out[block, :EARLY] = first.finish(block).astype(BF)
    second.late()
    late.left_first()
    plane.left_first()
    for copies in (line, plane, plane_sum, early, late, first, weights):
        copies.left()
    keep.wait()
    second.arrive()
    for block in (0, 1):
        back_out[block, EARLY:] = second.finish(block).astype(BF)
    second.left()


def finish_kernel(back, w_one, grads, input_grad, grad_one, grad_two):
    grad_one[...] = grads[:BS]
    grad_two[...] = grads[BS:]
    for block in (0, 1):
        input_grad[pl.ds(block * BS, BS)] = DOT(w_one[...], back[block]).T.astype(BF)


def write_plan(rows, cols, count, plan):
    shape = (SLOTS, SLOTS)
    down = lax.broadcasted_iota(jnp.int32, shape, 0)
    across = lax.broadcasted_iota(jnp.int32, shape, 1)
    live = down < count

    def tall(ref, top):
        return jnp.broadcast_to(jnp.clip(ref[...], 0, top), shape).T

    def over_slots(where, values):
        return jnp.sum(jnp.where(where, values, 0), axis=0, keepdims=True)

    rows, cols = tall(rows, ROW_UNITS - 1), tall(cols, COL_UNITS - 1)
    for at, last_at, major, minor in ((0, 6, rows, cols), (3, 8, cols, rows)):
        key = jnp.where(live, major * 64 + minor, 4096 + down)
        rank = jnp.sum(jnp.where(key.T < key, 1, 0), axis=1, keepdims=True)
        here = rank == across
        alive = jnp.where(live, major, -1)
        plan[at : at + 1] = over_slots(here, down)
        plan[at + 1 : at + 2] = over_slots(here, minor)
        same = over_slots(here, alive) == over_slots(rank + 1 == across, alive)
        plan[at + 2 : at + 3] = jnp.where(same & (across[:1] > 0), 1, 0)
        plan[last_at : last_at + 1] = jnp.maximum(over_slots(live & (major <= across), 1) - 1, 0)
        plan[last_at + 1 : last_at + 2] = jnp.minimum(over_slots(live & (major == across), 1), 1)


def units(count, rows=BS):
    return pltpu.VMEM((count, rows, BS), BF)


SMEM = pl.BlockSpec(memory_space=pltpu.SMEM)
VMEM = pl.BlockSpec(memory_space=pltpu.VMEM)
ANY = pl.BlockSpec(memory_space=pl.ANY)


def call(rows, cols, count, feats, cot, w_one, w_two, tiles):
    half = BS // 2

    def last(rows):
        return [units(ROW_UNITS, rows), units(8, rows), units(2, rows), units(4, rows)]

    return pl.pallas_call(
        kernel,
        out_shape=(
            jax.ShapeDtypeStruct((2, BS, BS), BF),
            jax.ShapeDtypeStruct((2, 4, 4, 16, BS), F32),
        ),
        in_specs=[ANY, ANY, SMEM, ANY, ANY, ANY, ANY, ANY],
        out_specs=(VMEM, ANY),
        scratch_shapes=[
            pltpu.VMEM((1, SLOTS), jnp.int32),
            pltpu.VMEM((1, SLOTS), jnp.int32),
            pltpu.VMEM((2 * BS, BS), BF),
            pltpu.VMEM((BS, BS), BF),
            pltpu.VMEM((BS, BS), BF),
            pltpu.SMEM((16, SLOTS), jnp.int32),
            pltpu.VMEM((16, SLOTS), jnp.int32),
            units(SLOTS),
            units(SLOTS),
            pltpu.VMEM((BS, BS), F32),
            units(COL_UNITS),
            units(ROW_UNITS),
            units(ROW_UNITS),
            units(16, half),
            units(16),
            units(8),
            units(4, half),
            units(4),
            units(COL_UNITS),
            units(8),
            units(2),
            units(4),
            pltpu.VMEM((BS, BS), BF),
            *last(EARLY),
            *last(BS - EARLY),
            pltpu.VMEM((2 * BS, BS), F32),
            pltpu.VMEM((BS, BS), F32),
            pltpu.VMEM((3, 64, BS), F32),
            pltpu.VMEM((3, 16, BS), F32),
            pltpu.VMEM((4, 16, BS), F32),
            pltpu.VMEM((2, 4, 4, 16, BS), F32),
            pltpu.SemaphoreType.DMA,
            pltpu.SemaphoreType.DMA,
            pltpu.SemaphoreType.DMA,
            pltpu.SemaphoreType.DMA((2,)),
            pltpu.SemaphoreType.DMA((4,)),
            pltpu.SemaphoreType.DMA,
            pltpu.SemaphoreType.DMA((76,)),
        ],
        compiler_params=pltpu.CompilerParams(
            collective_id=0, has_side_effects=True, vmem_limit_bytes=62 * 2**20
        ),
        name="graph_back",
    )(rows, cols, count, feats, cot, w_one, w_two, tiles)


def per_device(
    node_feats, out_grad, weight_one, weight_two, tile_values, tile_rows, tile_cols, tile_count
):
    back, grads = call(
        tile_rows.reshape(1, SLOTS),
        tile_cols.reshape(1, SLOTS),
        tile_count,
        node_feats,
        out_grad,
        weight_one,
        weight_two,
        tile_values,
    )
    return pl.pallas_call(
        finish_kernel,
        out_shape=(
            jax.ShapeDtypeStruct((2 * BS, BS), BF),
            jax.ShapeDtypeStruct((BS, BS), F32),
            jax.ShapeDtypeStruct((BS, BS), F32),
        ),
        in_specs=[VMEM, VMEM, VMEM],
        out_specs=(VMEM, VMEM, VMEM),
        name="finish",
    )(back, weight_one, grads.reshape(2 * BS, BS))


def solution(mesh):
    in_specs = (
        P(("row", "col"), None),
        P(("row", "col"), None),
        P(),
        P(),
        P(("row", "col"), None, None),
        P(("row", "col")),
        P(("row", "col")),
        P(("row", "col")),
    )
    out_specs = (P(("row", "col"), None), P(), P())
    return jax.shard_map(
        per_device, mesh=mesh, in_specs=in_specs, out_specs=out_specs, check_vma=False
    )
```

```python
import functools

import jax
import jax.numpy as jnp
from jax import lax
from jax.experimental import pallas as pl
from jax.experimental.pallas import tpu as pltpu
from jax.sharding import PartitionSpec as P

BF = jnp.bfloat16
F32 = jnp.float32
BS = 256
SLOTS = 128
ROW_UNITS = 32
COL_UNITS = 16
UNROLL = 32
EARLY = 128
WAYS = (1, -1)
DOT = functools.partial(jnp.dot, preferred_element_type=F32)
ROWS_OF_HALF = {1: 0, -1: 1}
PARTNERS = [(axis, step) for axis in ("x", "y", "z") for step in (1, -1, 2)] + [("core", 0)]


class Net:
    def __init__(self, sems):
        self.sems = sems
        row, col = lax.axis_index("row"), lax.axis_index("col")
        self.at = {"x": row // 2, "y": col // 4, "z": col % 4}
        self.core = row % 2
        self.keys = {}

    def off(self, axis, step):
        return (self.at[axis] + (step + 4)) % 4

    def peer(self, axis, step):
        at = dict(self.at)
        core = self.core
        if axis == "core":
            core = 1 - core
        else:
            at[axis] = self.off(axis, step)
        return (at["x"] * 2 + core, at["y"] * 4 + at["z"])

    def greet(self):
        barrier = pltpu.get_barrier_semaphore()
        for axis, way in PARTNERS:
            pl.semaphore_signal(
                barrier, inc=1, device_id=self.peer(axis, way), device_id_type=pl.DeviceIdType.MESH
            )

    def met(self):
        pl.semaphore_wait(pltpu.get_barrier_semaphore(), len(PARTNERS))

    def copy(self, leave, land, src, dst, axis, way):
        at = [self.keys.setdefault(key, len(self.keys)) for key in (("out", leave), ("in", land))]
        return pltpu.make_async_remote_copy(
            src_ref=src,
            dst_ref=dst,
            send_sem=self.sems.at[at[0]],
            recv_sem=self.sems.at[at[1]],
            device_id=self.peer(axis, way),
            device_id_type=pl.DeviceIdType.MESH,
        )

    def send(self, leave, land, src, dst, axis, way):
        self.copy(leave, land, src, dst, axis, way).start()

    def got(self, leave, land, ref):
        self.copy(leave, land, ref, ref, "core", 0).wait_recv()

    def left(self, leave, land, ref):
        self.copy(leave, land, ref, ref, "core", 0).wait_send()


class GatherPlane:
    def __init__(self, net, tag, buf):
        self.net, self.tag, self.buf = net, tag, buf
        self.half_rows = buf.shape[1] // 2

    def axes(self, block):
        return ("y", "z") if block == 0 else ("z", "y")

    def unit(self, block, first, second):
        one, two = self.axes(block)
        at = {one: self.net.off(one, first), two: self.net.off(two, second)}
        return (at["y"] * 4 + at["z"]) * 2 + block

    def whole(self, block, first, second):
        return self.buf.at[self.unit(block, first, second)]

    def half(self, block, first, second, way):
        rows = pl.ds(ROWS_OF_HALF[way] * self.half_rows, self.half_rows)
        return self.buf.at[self.unit(block, first, second), rows]

    def put(self, key, ref, axis, way):
        leave = (self.tag, "a" if key == ("a",) else "rest")
        self.net.send(leave, (self.tag, *key), ref, ref, axis, way)

    def get(self, key, count):
        self.net.got((self.tag, "a"), (self.tag, *key), self.buf.at[pl.ds(0, count)])

    def spread(self, block, first):
        two = self.axes(block)[1]
        for way in WAYS:
            self.put(("c", first), self.whole(block, first, 0), two, way)

    def start(self):
        for block in (0, 1):
            one = self.axes(block)[0]
            for way in WAYS:
                self.put(("a",), self.whole(block, 0, 0), one, way)

    def start_more(self):
        for block in (0, 1):
            self.spread(block, 0)

    def step1(self):
        self.get(("a",), 4)
        for block in (0, 1):
            one = self.axes(block)[0]
            for way in WAYS:
                self.put(("f",), self.half(block, -way, 0, way), one, way)
        for way in WAYS:
            for block in (0, 1):
                self.spread(block, -way)

    def pass_on(self, first):
        self.get(("c", first), 4)
        for block in (0, 1):
            two = self.axes(block)[1]
            for way in WAYS:
                self.put(("e",), self.half(block, first, -way, way), two, way)

    def step2(self):
        self.pass_on(0)

    def step3(self):
        self.get(("f",), 2)
        for block in (0, 1):
            self.spread(block, 2)

    def step4(self):
        self.pass_on(-1)
        self.pass_on(1)

    def step5(self):
        self.pass_on(2)

    def finish(self):
        self.get(("e",), 8)

    def left_first(self):
        self.net.left((self.tag, "a"), (self.tag, "a"), self.buf.at[pl.ds(0, 4)])

    def left(self):
        self.net.left((self.tag, "rest"), (self.tag, "a"), self.buf.at[pl.ds(0, 26)])


class GatherLine:
    def __init__(self, net, tag, buf):
        self.net, self.tag, self.buf = net, tag, buf

    def first(self, step, core):
        return (self.net.off("x", step) * 2 + core) * 2

    def get(self, kind, count):
        self.net.got(self.tag, (self.tag, kind), self.buf.at[pl.ds(0, count)])

    def share(self, step):
        ref = self.buf.at[pl.ds(self.first(step, self.net.core), 2)]
        self.net.send(self.tag, (self.tag, "s"), ref, ref, "core", 0)

    def pass_half(self, kind, step, h, way):
        ref = self.buf.at[self.first(step, self.net.core) + h]
        self.net.send(self.tag, (self.tag, kind), ref, ref, "x", way)

    def start(self):
        for way in WAYS:
            self.pass_half("a", 0, ROWS_OF_HALF[way], way)

    def start_more(self):
        for way in WAYS:
            self.pass_half("b", 0, 1 - ROWS_OF_HALF[way], way)
        self.share(0)

    def step1(self):
        self.get("a", 2)
        for way in WAYS:
            self.pass_half("f", -way, ROWS_OF_HALF[way], way)

    def step2(self):
        self.get("b", 2)
        for way in WAYS:
            self.share(-way)

    def step3(self):
        self.get("f", 2)
        self.share(2)

    def finish(self):
        self.get("s", 8)

    def left(self):
        self.net.left(self.tag, (self.tag, "a"), self.buf.at[pl.ds(0, 14)])


class RingSum:
    def __init__(self, net, tag, keys, axis, half, relay, landed, more=None):
        self.net, self.tag, self.keys, self.axis = net, tag, keys, axis
        self.half, self.relay, self.landed, self.more = half, relay, landed, more

    def send(self, at, src, dst, way):
        self.net.send((self.tag, at), self.keys[at], src, dst, self.axis, way)

    def term(self, step, h):
        value = self.half(step, h)[...].astype(F32)
        return value if self.more is None else value + self.more(step, h)[...].astype(F32)

    def start(self):
        for way in WAYS:
            self.send(0, self.half(2, ROWS_OF_HALF[way]), self.relay[way], way)

    def start_near(self):
        for way in WAYS:
            rest = 1 - ROWS_OF_HALF[way]
            self.send(1, self.half(way, rest), self.landed[way][rest], way)

    def middle(self):
        for way in WAYS:
            turn = ROWS_OF_HALF[way]
            mine = self.half(way, turn)
            mine[...] = (self.term(way, turn) + self.relay[way][...].astype(F32)).astype(BF)
            self.send(1, mine, self.landed[way][turn], way)

    def finish(self, h):
        total = self.term(0, h)
        for way in WAYS:
            total = total + self.landed[way][h][...].astype(F32)
        return total


class LineSum:
    def __init__(self, net, tag, part, swapped, relay, landed):
        self.net, self.tag, self.part, self.swapped = net, tag, part, swapped
        self.relay, self.landed = relay, landed
        self.ring = RingSum(
            net,
            tag,
            ((tag, "p"), (tag, "n")),
            "x",
            lambda step, h: part.at[self.first(step, net.core) + h],
            {1: relay.at[0], -1: relay.at[1]},
            {1: [landed.at[0], landed.at[1]], -1: [landed.at[2], landed.at[3]]},
            lambda step, h: swapped.at[net.off("x", step) * 2 + h],
        )

    def first(self, step, core):
        return (self.net.off("x", step) * 2 + core) * 2

    def get(self, kind, ref):
        self.net.got((self.tag, 0), (self.tag, kind), ref)

    def start(self):
        for step in (2, 1, -1, 0):
            src = self.part.at[pl.ds(self.first(step, 1 - self.net.core), 2)]
            dst = self.swapped.at[pl.ds(self.net.off("x", step) * 2, 2)]
            self.net.send((self.tag, 1), (self.tag, "s" if step == 2 else "u"), src, dst, "core", 0)

    def join(self, step, h):
        self.part[self.first(step, self.net.core) + h] = self.ring.term(step, h).astype(BF)

    def middle(self):
        self.get("s", self.swapped.at[pl.ds(0, 2)])
        self.join(2, 0)
        self.join(2, 1)
        self.ring.start()

    def middle_more(self):
        self.get("u", self.swapped.at[pl.ds(0, 6)])
        for way in WAYS:
            self.join(way, 1 - ROWS_OF_HALF[way])

    def near(self):
        self.net.left((self.tag, 0), (self.tag, "s"), self.relay)
        self.ring.start_near()

    def late(self):
        self.get("p", self.relay)
        self.ring.middle()

    def arrive(self):
        self.get("n", self.landed)

    def finish(self, h):
        return self.ring.finish(h)

    def left(self):
        self.net.left((self.tag, 1), (self.tag, "s"), self.part.at[pl.ds(0, 12)])


class PlaneSum:
    ORDER = (2, 1, -1, 0)

    def __init__(self, net, tag, part, relay, landed, part2, relay2, landed2):
        self.net, self.tag, self.part, self.part2 = net, tag, part, part2
        rows = part.shape[1] // 2
        cut = [pl.ds(0, rows), pl.ds(rows, rows)]
        self.cut = cut
        self.rings, self.last = {}, {}
        for block in (0, 1):
            one, two = ("z", "y") if block == 0 else ("y", "z")

            def unit(first, second, block=block, one=one, two=two):
                at = {one: net.off(one, first), two: net.off(two, second)}
                return (at["y"] * 4 + at["z"]) * 2 + block

            for k, second in enumerate(self.ORDER):
                base = (block * 4 + k) * 2
                self.rings[block, k] = RingSum(
                    net,
                    tag,
                    ((tag, "p", k), (tag, "n", k)),
                    one,
                    lambda step, h, unit=unit, second=second: part.at[unit(step, second), cut[h]],
                    {1: relay.at[base], -1: relay.at[base + 1]},
                    {
                        1: [landed.at[base, cut[h]] for h in (0, 1)],
                        -1: [landed.at[base + 1, cut[h]] for h in (0, 1)],
                    },
                )
            base = block * 2
            self.last[block] = RingSum(
                net,
                tag,
                ((tag, "p", 4), (tag, "n", 4)),
                two,
                lambda step, h, block=block: part2.at[block * 4 + self.ORDER.index(step), cut[h]],
                {1: relay2.at[base], -1: relay2.at[base + 1]},
                {
                    1: [landed2.at[base, cut[h]] for h in (0, 1)],
                    -1: [landed2.at[base + 1, cut[h]] for h in (0, 1)],
                },
            )

    def get(self, kind, k, count):
        self.net.got((self.tag, 0), (self.tag, kind, k), self.part.at[pl.ds(0, count)])

    def start(self, k):
        for block in (0, 1):
            self.rings[block, k].start()

    def start_near(self, k):
        for block in (0, 1):
            self.rings[block, k].start_near()

    def middle(self, k):
        self.get("p", k, 2)
        for block in (0, 1):
            self.rings[block, k].middle()

    def close(self, k):
        self.get("n", k, 4)
        for block in (0, 1):
            for h in (0, 1):
                self.part2[block * 4 + k, self.cut[h]] = self.rings[block, k].finish(h).astype(BF)
        if k == 0:
            for block in (0, 1):
                self.last[block].start()
        if k == 2:
            for block in (0, 1):
                self.last[block].start_near()

    def late(self):
        self.get("p", 4, 2)
        for block in (0, 1):
            self.last[block].middle()

    def arrive(self):
        self.get("n", 4, 4)

    def finish(self, block, h):
        return self.last[block].finish(h)

    def left(self):
        self.net.left((self.tag, 0), (self.tag, "p", 0), self.part.at[pl.ds(0, 10)])
        self.net.left((self.tag, 1), (self.tag, "p", 0), self.part.at[pl.ds(0, 20)])


class GradSum:
    FAR = (1, -1, 2)

    def __init__(self, net, mine, swapped, from_x, from_y, from_z, done):
        self.net, self.mine, self.swapped, self.done = net, mine, swapped, done
        self.from_x, self.from_y, self.from_z = from_x, from_y, from_z

    def rows(self, *steps):
        size = {1: 256, 2: 64, 3: 16}[len(steps)]
        at = ((1 - self.net.core) if steps[0] else self.net.core) * 256
        for axis, step, span in zip(("x", "y"), steps[1:], (64, 16)):
            at = at + self.net.off(axis, step) * span
        return pl.ds(pl.multiple_of(at, size), size)

    def put(self, stage, src, dst, axis, step):
        self.net.send(("w", axis), ("w", stage), src, dst, axis, step)

    def get(self, stage, ref):
        self.net.got(("w", "core"), ("w", stage), ref)

    def start(self):
        self.put(0, self.mine.at[self.rows(1)], self.swapped, "core", 0)

    def step1(self):
        self.get(0, self.swapped)
        rows = self.rows(0)
        self.mine[rows] = self.mine[rows] + self.swapped[...]
        for k, step in enumerate(self.FAR):
            self.put(1, self.mine.at[self.rows(0, step)], self.from_x.at[k], "x", step)

    def step2(self):
        self.get(1, self.from_x)
        rows = self.rows(0, 0)
        self.mine[rows] = (self.mine[rows] + self.from_x[0]) + (self.from_x[1] + self.from_x[2])
        for k, step in enumerate(self.FAR):
            self.put(2, self.mine.at[self.rows(0, 0, step)], self.from_y.at[k], "y", step)

    def step3(self):
        self.get(2, self.from_y)
        ref = self.from_z.at[self.net.at["z"]]
        ref[...] = (self.mine[self.rows(0, 0, 0)] + self.from_y[0]) + (self.from_y[1] + self.from_y[2])
        for step in self.FAR:
            self.put(3, ref, ref, "z", step)

    def step4(self):
        self.get(3, self.from_z.at[pl.ds(0, 3)])
        at = self.net.at
        ref = self.done.at[self.net.core, at["x"], at["y"]]
        ref[...] = (self.from_z[0] + self.from_z[1]) + (self.from_z[2] + self.from_z[3])
        for step in self.FAR:
            self.put(4, ref, ref, "x", step)

    def step5(self):
        self.get(4, self.from_y)
        ref = self.done.at[self.net.core, :, self.net.at["y"]]
        for step in self.FAR:
            self.put(5, ref, ref, "y", step)

    def step6(self):
        self.get(5, self.from_x)
        ref = self.done.at[self.net.core]
        self.put(6, ref, ref, "core", 0)

    def finish(self):
        self.get(6, self.swapped)

    def left(self):
        for axis, rows in (("core", 512), ("x", 240), ("y", 240), ("z", 48)):
            self.net.left(("w", axis), ("w", 0), self.mine.at[pl.ds(0, rows)])


def within(index, count):
    return jnp.clip(index, 0, count - 1)


def products(count, begin, left, right, keep, total, sums, unroll=UNROLL):
    def body(step, carry):
        for turn in range(unroll):
            t = begin + step * unroll + turn
            value = total[...] * keep(t) + DOT(left(t), right(t))
            total[...] = value
            sums[t] = value.astype(BF)
        return carry

    lax.fori_loop(0, count // unroll, body, 0)


def pick(units, sums, last, some, part):
    def body(u, carry):
        part[u] = (sums[last(u)].astype(F32) * some(u)).astype(BF)
        return carry

    lax.fori_loop(0, units, body, 0)


def both(values):
    high = values.astype(BF)
    return high, (values - high.astype(F32)).astype(BF)


NT = (((1,), (1,)), ((), ()))


def kernel(
    rows_in, cols_in, count, feats, cot_in, w_one_in, w_two_in, tiles_hbm, back_out, grads_out,
    rows, cols, cot, w_one, w_two, plan, plan_wide, tiles, sums, total, feats_all, cot_all, part, relay, landed, part2, relay2, landed2,
    part_x, swapped, relay_x, landed_x, w_one_t,
    slope_all_0, swapped_0, relay_0, landed_0,
    slope_all_1, swapped_1, relay_1, landed_1,
    mine, swapped_w, from_x, from_y, from_z, done, tile_sem, plan_sem, cot_sem, feats_sem, small_sem, grads_sem, sems,
):
    net = Net(sems)
    net.greet()
    line = GatherLine(net, "x", feats_all)
    plane = GatherPlane(net, "g", cot_all)
    loads = [pltpu.make_async_copy(cot_in, cot, cot_sem)]
    for block in (0, 1):
        span = pl.ds(block * BS, BS)
        own = feats_all.at[line.first(0, net.core) + block]
        loads.append(pltpu.make_async_copy(feats.at[span], own, feats_sem.at[block]))
    for at, (src, dst) in enumerate(((rows_in, rows), (cols_in, cols), (w_one_in, w_one), (w_two_in, w_two))):
        loads.append(pltpu.make_async_copy(src, dst, small_sem.at[at]))
    loads.append(pltpu.make_async_copy(tiles_hbm, tiles, tile_sem))
    for load in loads:
        load.start()
    loads[0].wait()
    for block in (0, 1):
        span = pl.ds(block * BS, BS)
        cot_all[plane.unit(block, 0, 0)] = cot[span].astype(F32).T.astype(BF)
    for load in loads[1:-1]:
        load.wait()
    w_one_t[...] = w_one[...].astype(F32).T.astype(BF)
    total[...] = jnp.zeros_like(total)
    write_plan(rows, cols, count[0], plan_wide)
    to_plan = pltpu.make_async_copy(plan_wide, plan, plan_sem)
    to_plan.start()
    net.met()
    line.start()
    plane.start()
    line.start_more()
    plane.start_more()
    line.step1()
    plane.step1()
    line.step2()
    plane.step2()
    line.step3()
    line.finish()
    loads[-1].wait()
    to_plan.wait()

    def ahead(count, begin):
        products(
            count,
            begin,
            lambda t: tiles[within(plan[0, t], SLOTS)],
            lambda t: feats_all[within(plan[1, t], COL_UNITS)],
            lambda t: plan[2, t].astype(F32),
            total,
            sums,
        )

    def back(count, begin, left, rows, unroll=UNROLL):
        products(
            count,
            begin,
            lambda t: left[within(plan[4, t], ROW_UNITS)],
            lambda t: tiles[within(plan[3, t], SLOTS)],
            lambda t: plan[5, t].astype(F32),
            total.at[pl.ds(0, rows)],
            sums.at[:, pl.ds(0, rows)],
            unroll,
        )

    def choose(to, rows):
        pick(
            COL_UNITS,
            sums.at[:, pl.ds(0, rows)],
            lambda u: within(plan[8, u], SLOTS),
            lambda u: plan[9, u].astype(F32),
            to,
        )

    ahead(64, 0)
    plane.step3()
    ahead(64, 64)
    plane.step4()
    pick(ROW_UNITS, sums, lambda u: within(plan[6, u], SLOTS), lambda u: plan[7, u].astype(F32), part)
    plane_sum = PlaneSum(net, "ax", part, relay, landed, part2, relay2, landed2)
    plane_sum.start(0)
    plane.step5()
    plane_sum.start_near(0)
    plane_sum.start(1)
    plane_sum.start(2)
    total[...] = jnp.zeros_like(total)
    plane.finish()
    plane_sum.start_near(1)
    plane_sum.start_near(2)
    back(64, 0, cot_all, BS)
    plane_sum.middle(0)
    plane_sum.start(3)
    plane_sum.start_near(3)
    back(64, 64, cot_all, BS)
    choose(part_x, BS)
    line_sum = LineSum(net, "bt", part_x, swapped, relay_x, landed_x)
    line_sum.start()
    plane_sum.middle(1)
    plane_sum.middle(2)
    line_sum.middle()
    line_sum.middle_more()
    plane_sum.close(0)
    plane_sum.middle(3)
    line_sum.near()
    plane_sum.close(1)
    line_sum.late()
    plane_sum.close(2)
    plane_sum.late()
    plane_sum.close(3)
    line_sum.arrive()
    plane_sum.arrive()
    early = GatherPlane(net, "p", slope_all_0)
    late = GatherPlane(net, "q", slope_all_1)
    ax_parts, hiddens, grads, back_two = [], [], [], []
    for block in (0, 1):
        back_two.append(line_sum.finish(block).astype(BF))
        d_hidden = DOT(w_two[...], back_two[block])
        ax = jnp.concatenate([plane_sum.finish(block, h) for h in (0, 1)], axis=0).T
        high, low = both(ax)
        pre = DOT(w_one_t[...], high) + DOT(w_one_t[...], low)
        gate = 1.0 / (1.0 + jnp.exp(-pre))
        slope = (d_hidden * gate * (1.0 + pre * (1.0 - gate))).astype(BF)
        grads.append(slope)
        slope_all_0[early.unit(block, 0, 0)] = slope[:EARLY]
        slope_all_1[late.unit(block, 0, 0)] = slope[EARLY:]
        hiddens.append((pre * gate).astype(BF))
        ax_parts.append((high, low))
    early.start()
    total[...] = jnp.zeros_like(total)
    one = jnp.zeros((BS, BS), F32)
    two = jnp.zeros((BS, BS), F32)
    for block in (0, 1):
        two += lax.dot_general(hiddens[block], back_two[block], NT, preferred_element_type=F32)
        for values in ax_parts[block]:
            one += lax.dot_general(values, grads[block], NT, preferred_element_type=F32)
    mine[:BS] = one
    mine[BS:] = two
    weights = GradSum(net, mine, swapped_w, from_x, from_y, from_z, done)
    weights.start()
    early.left_first()
    early.start_more()
    late.start()
    weights.step1()
    early.step1()
    early.step2()
    weights.step2()
    late.start_more()
    early.step3()
    early.step4()
    late.step1()
    early.step5()
    weights.step3()
    late.step2()
    late.step3()
    late.step4()
    early.finish()
    back(32, 0, slope_all_0, EARLY, 32)
    late.step5()
    weights.step4()
    back(96, 32, slope_all_0, EARLY, 32)
    line_sum.left()
    part_0, part_1 = part_x.at[:, pl.ds(0, EARLY)], part_x.at[:, pl.ds(EARLY, BS - EARLY)]
    choose(part_0, EARLY)
    first = LineSum(net, "s", part_0, swapped_0, relay_0, landed_0)
    second = LineSum(net, "t", part_1, swapped_1, relay_1, landed_1)
    first.start()
    total[...] = jnp.zeros_like(total)
    late.finish()
    back(32, 0, slope_all_1, BS - EARLY, 32)
    weights.step5()
    first.middle()
    first.middle_more()
    back(64, 32, slope_all_1, BS - EARLY, 32)
    first.near()
    back(32, 96, slope_all_1, BS - EARLY, 32)
    choose(part_1, BS - EARLY)
    second.start()
    first.late()
    second.middle()
    second.middle_more()
    second.near()
    weights.step6()
    first.arrive()
    for block in (0, 1):
        back_out[block, :EARLY] = first.finish(block).astype(BF)
    second.late()
    weights.finish()
    keep = pltpu.make_async_copy(done, grads_out, grads_sem)
    keep.start()
    late.left_first()
    plane.left_first()
    for copies in (line, plane, plane_sum, early, late, first, weights):
        copies.left()
    keep.wait()
    second.arrive()
    for block in (0, 1):
        back_out[block, EARLY:] = second.finish(block).astype(BF)
    second.left()


def finish_kernel(back, w_one, grads, input_grad, grad_one, grad_two):
    grad_one[...] = grads[:BS]
    grad_two[...] = grads[BS:]
    for block in (0, 1):
        input_grad[pl.ds(block * BS, BS)] = DOT(w_one[...], back[block]).T.astype(BF)


def write_plan(rows, cols, count, plan):
    shape = (SLOTS, SLOTS)
    down = lax.broadcasted_iota(jnp.int32, shape, 0)
    across = lax.broadcasted_iota(jnp.int32, shape, 1)
    live = down < count

    def tall(ref, top):
        return jnp.broadcast_to(jnp.clip(ref[...], 0, top), shape).T

    def over_slots(where, values):
        return jnp.sum(jnp.where(where, values, 0), axis=0, keepdims=True)

    rows, cols = tall(rows, ROW_UNITS - 1), tall(cols, COL_UNITS - 1)
    for at, last_at, major, minor in ((0, 6, rows, cols), (3, 8, cols, rows)):
        key = jnp.where(live, major * 64 + minor, 4096 + down)
        rank = jnp.sum(jnp.where(key.T < key, 1, 0), axis=1, keepdims=True)
        here = rank == across
        alive = jnp.where(live, major, -1)
        plan[at : at + 1] = over_slots(here, down)
        plan[at + 1 : at + 2] = over_slots(here, minor)
        same = over_slots(here, alive) == over_slots(rank + 1 == across, alive)
        plan[at + 2 : at + 3] = jnp.where(same & (across[:1] > 0), 1, 0)
        plan[last_at : last_at + 1] = jnp.maximum(over_slots(live & (major <= across), 1) - 1, 0)
        plan[last_at + 1 : last_at + 2] = jnp.minimum(over_slots(live & (major == across), 1), 1)


def units(count, rows=BS):
    return pltpu.VMEM((count, rows, BS), BF)


SMEM = pl.BlockSpec(memory_space=pltpu.SMEM)
VMEM = pl.BlockSpec(memory_space=pltpu.VMEM)
ANY = pl.BlockSpec(memory_space=pl.ANY)


def call(rows, cols, count, feats, cot, w_one, w_two, tiles):
    half = BS // 2

    def last(rows):
        return [units(ROW_UNITS, rows), units(8, rows), units(2, rows), units(4, rows)]

    return pl.pallas_call(
        kernel,
        out_shape=(
            jax.ShapeDtypeStruct((2, BS, BS), BF),
            jax.ShapeDtypeStruct((2, 4, 4, 16, BS), F32),
        ),
        in_specs=[ANY, ANY, SMEM, ANY, ANY, ANY, ANY, ANY],
        out_specs=(VMEM, ANY),
        scratch_shapes=[
            pltpu.VMEM((1, SLOTS), jnp.int32),
            pltpu.VMEM((1, SLOTS), jnp.int32),
            pltpu.VMEM((2 * BS, BS), BF),
            pltpu.VMEM((BS, BS), BF),
            pltpu.VMEM((BS, BS), BF),
            pltpu.SMEM((16, SLOTS), jnp.int32),
            pltpu.VMEM((16, SLOTS), jnp.int32),
            units(SLOTS),
            units(SLOTS),
            pltpu.VMEM((BS, BS), F32),
            units(COL_UNITS),
            units(ROW_UNITS),
            units(ROW_UNITS),
            units(16, half),
            units(16),
            units(8),
            units(4, half),
            units(4),
            units(COL_UNITS),
            units(8),
            units(2),
            units(4),
            pltpu.VMEM((BS, BS), BF),
            *last(EARLY),
            *last(BS - EARLY),
            pltpu.VMEM((2 * BS, BS), F32),
            pltpu.VMEM((BS, BS), F32),
            pltpu.VMEM((3, 64, BS), F32),
            pltpu.VMEM((3, 16, BS), F32),
            pltpu.VMEM((4, 16, BS), F32),
            pltpu.VMEM((2, 4, 4, 16, BS), F32),
            pltpu.SemaphoreType.DMA,
            pltpu.SemaphoreType.DMA,
            pltpu.SemaphoreType.DMA,
            pltpu.SemaphoreType.DMA((2,)),
            pltpu.SemaphoreType.DMA((4,)),
            pltpu.SemaphoreType.DMA,
            pltpu.SemaphoreType.DMA((76,)),
        ],
        compiler_params=pltpu.CompilerParams(
            collective_id=0, has_side_effects=True, vmem_limit_bytes=62 * 2**20
        ),
        name="graph_back",
    )(rows, cols, count, feats, cot, w_one, w_two, tiles)


def per_device(
    node_feats, out_grad, weight_one, weight_two, tile_values, tile_rows, tile_cols, tile_count
):
    back, grads = call(
        tile_rows.reshape(1, SLOTS),
        tile_cols.reshape(1, SLOTS),
        tile_count,
        node_feats,
        out_grad,
        weight_one,
        weight_two,
        tile_values,
    )
    return pl.pallas_call(
        finish_kernel,
        out_shape=(
            jax.ShapeDtypeStruct((2 * BS, BS), BF),
            jax.ShapeDtypeStruct((BS, BS), F32),
            jax.ShapeDtypeStruct((BS, BS), F32),
        ),
        in_specs=[VMEM, VMEM, VMEM],
        out_specs=(VMEM, VMEM, VMEM),
        name="finish",
    )(back, weight_one, grads.reshape(2 * BS, BS))


def solution(mesh):
    in_specs = (
        P(("row", "col"), None),
        P(("row", "col"), None),
        P(),
        P(),
        P(("row", "col"), None, None),
        P(("row", "col")),
        P(("row", "col")),
        P(("row", "col")),
    )
    out_specs = (P(("row", "col"), None), P(), P())
    return jax.shard_map(
        per_device, mesh=mesh, in_specs=in_specs, out_specs=out_specs, check_vma=False
    )
```
